32 devices in a mesh: row: 4 (over y, core), col: 2 (over x), rep: 4 (over z).
Axes of the slice: x: 2, y: 2, z: 4, core: 2. Of those that a mesh axis runs over, the one named last changes fastest.
Arguments:
- features: float32 [256, 4096], P('rep', ('col', 'row')), may hold values from -6 to 6
- weight: float32 [256, 256], replicated, may hold values from -0.375 to 0.375
- cotangent: float32 [256, 4096], P('rep', ('row', 'col')), may hold values from -6 to 6
- tile_values: float32 [1280, 128, 128], P(('row', 'col')), may hold values from -0.078125 to 0.078125
- tile_row: int32 [1280], P(('row', 'col')), may hold values from 0 to 7
- tile_col: int32 [1280], P(('row', 'col')), may hold values from 0 to 15
- tile_kind: int32 [1280], P(('row', 'col')), may hold values from 0 to 159
- tile_count: int32 [8], P(('row', 'col')), may hold values from 40 to 160, as said below
Outputs:
- output: float32 [256, 4096], P('rep', ('row', 'col'))
- input_grad: float32 [256, 4096], P('rep', ('col', 'row'))
- weight_grad: float32 [256, 256], P('rep')
The draws below stay inside these ranges and needn't reach their ends.
Inputs may be any that keep to these rules, and one draw needn't show every extreme that they name: `tile_count`: a block's slots at or after its count are not part of the adjacency; some block uses all 160 slots. `tile_row`: slots may repeat a tile position; their tiles add. `tile_kind`: an index into the 160 stored tiles of the same block.
All inputs are finite; a program needn't handle non-finite values.
Results may differ from the reference program's by a relative error of at most 0.0001.
Values sent between devices are 32-bit elements; how exact they have to be, the bound alone decides.
A program may use at most 128 MiB of HBM per device.

```python
import jax
import jax.numpy as jnp
from jax import lax

F = 256
TILE = 128
CT = 4
TD = 160
BLOCKS = 8
NODES = 4096
N_ROW = 4
N_COL = 2


def draw_tile_count(key, part):
    lowest = max(TD // 4, 1)
    counts = jax.random.randint(key, (BLOCKS,), lowest, TD + 1)
    fullest = jax.random.randint(jax.random.fold_in(key, 7), (), 0, BLOCKS)
    return jnp.where(jnp.arange(BLOCKS) == fullest, TD, counts).astype(jnp.int32)


def place_ends(drawn, own_key, least, largest):
    longest = drawn.shape.index(max(drawn.shape))
    spots = []
    for shift in (0, 1):
        where = [jax.random.randint(jax.random.fold_in(own_key, axis), (), 0, length) for axis, length in enumerate(drawn.shape)]
        where[longest] = (where[longest] + shift) % drawn.shape[longest]
        spots.append(tuple(where))
    return drawn.at[spots[0]].set(least).at[spots[1]].set(largest)


def block_scale(key, shape, cuts, low, high):
    loudness, own = 1.0, jax.random.fold_in(key, 6)
    for position, parts in cuts:
        steps = jnp.exp(jax.random.uniform(jax.random.fold_in(own, position), (parts,), jnp.float32, low / len(cuts), high / len(cuts)))
        loudness = loudness * jnp.repeat(steps, shape[position] // parts).reshape([-1 if axis == position else 1 for axis in range(len(shape))])
    return loudness


def bell_draw(own_key, extent, width, reach, shards=(), kind=jnp.bfloat16):
    level = block_scale(own_key, extent, shards, -0.22, 0.18) if shards else 1.0
    drawn = jax.random.normal(own_key, extent, jnp.float32) * width * level
    return jnp.minimum(jnp.maximum(drawn, -reach), reach).astype(kind)


def setup_inputs(seed: int = 0) -> dict:
    streams_of = jax.random.split(jax.random.key(seed), 9)
    features = bell_draw(streams_of[0], (F, NODES), 1.0, 6.0, ((0, 4), (1, 8)), jnp.float32)
    weight = bell_draw(streams_of[1], (F, F), F ** -0.5, 0.375, (), jnp.float32)
    cotangent = bell_draw(streams_of[2], (F, NODES), 1.0, 6.0, ((0, 4), (1, 8)), jnp.float32)
    tile_values = bell_draw(streams_of[3], (BLOCKS * TD, TILE, TILE), (TD * TILE // CT) ** -0.5, 0.078125, ((0, 8),), jnp.float32)
    tile_row = place_ends(jax.random.randint(streams_of[4], (BLOCKS * TD,), 0, N_COL * CT), jax.random.fold_in(streams_of[4], 1), 0, (N_COL * CT) - 1).astype(jnp.int32)
    tile_col = place_ends(jax.random.randint(streams_of[5], (BLOCKS * TD,), 0, N_ROW * CT), jax.random.fold_in(streams_of[5], 1), 0, (N_ROW * CT) - 1).astype(jnp.int32)
    tile_kind = place_ends(jax.random.randint(streams_of[6], (BLOCKS * TD,), 0, TD), jax.random.fold_in(streams_of[6], 1), 0, TD - 1).astype(jnp.int32)
    tile_count = draw_tile_count(jax.random.fold_in(streams_of[8], 71), 0)
    return dict(features=features, weight=weight, cotangent=cotangent, tile_values=tile_values, tile_row=tile_row, tile_col=tile_col, tile_kind=tile_kind, tile_count=tile_count)


def tile_terms(source, values, from_tile, to_tile, tile_kinds, live_weight, dest_tiles, transposed):
    feat_width = source.shape[0]
    tile_edge = values.shape[1]
    tiled = source.reshape(feat_width, source.shape[1] // tile_edge, tile_edge)
    picked = jnp.take(tiled, from_tile, axis=1)
    chosen = jnp.take(values, tile_kinds, axis=0)
    if transposed:
        products = jnp.einsum('fga,gab->fgb', picked, chosen, precision=lax.Precision.HIGHEST)
    else:
        products = jnp.einsum('fgb,gab->fga', picked, chosen, precision=lax.Precision.HIGHEST)
    onehot = (to_tile[:, None] == jnp.arange(dest_tiles, dtype=jnp.int32)[None, :]).astype(jnp.float32)
    onehot = onehot * live_weight[:, None]
    spread = jnp.einsum('fgt,gd->fdt', products, onehot, precision=lax.Precision.HIGHEST)
    return spread.reshape(feat_width, dest_tiles * tile_edge)

def reference(features, weight, cotangent, tile_values, tile_row, tile_col, tile_kind, tile_count):
    stretch_len = CT * TILE
    row_span = N_COL * stretch_len
    col_span = N_ROW * stretch_len
    mixed = jnp.dot(weight.T, features, preferred_element_type=jnp.float32, precision=lax.Precision.HIGHEST)
    pre = jnp.zeros_like(mixed)
    slot_ids = jnp.arange(TD, dtype=jnp.int32)
    for row_block in range(N_ROW):
        for col_block in range(N_COL):
            block_id = row_block * N_COL + col_block
            lower = block_id * TD
            live_weight = (slot_ids < tile_count[block_id]).astype(jnp.float32)
            values = tile_values[lower:lower + TD]
            source = mixed[:, col_block * col_span:(col_block + 1) * col_span]
            terms = tile_terms(source, values, tile_col[lower:lower + TD], tile_row[lower:lower + TD], tile_kind[lower:lower + TD], live_weight, N_COL * CT, False)
            pre = pre.at[:, row_block * row_span:(row_block + 1) * row_span].add(terms)
    output, pullback = jax.vjp(lambda v: jax.nn.gelu(v, approximate=True), pre)
    grad_pre, = pullback(cotangent)
    grad_mixed = jnp.zeros_like(mixed)
    for row_block in range(N_ROW):
        for col_block in range(N_COL):
            block_id = row_block * N_COL + col_block
            lower = block_id * TD
            live_weight = (slot_ids < tile_count[block_id]).astype(jnp.float32)
            values = tile_values[lower:lower + TD]
            source = grad_pre[:, row_block * row_span:(row_block + 1) * row_span]
            terms = tile_terms(source, values, tile_row[lower:lower + TD], tile_col[lower:lower + TD], tile_kind[lower:lower + TD], live_weight, N_ROW * CT, True)
            grad_mixed = grad_mixed.at[:, col_block * col_span:(col_block + 1) * col_span].add(terms)
    input_grad = jnp.dot(weight, grad_mixed, preferred_element_type=jnp.float32, precision=lax.Precision.HIGHEST)
    weight_grad = jnp.dot(features, grad_mixed.T, preferred_element_type=jnp.float32, precision=lax.Precision.HIGHEST)
    weight_grad = weight_grad * float(NODES) ** (-0.5)
    return (output, input_grad, weight_grad)
```

```python
import functools

import jax
import jax.numpy as jnp
from jax import lax
from jax.experimental import pallas as pl
from jax.experimental.pallas import tpu as pltpu
from jax.sharding import PartitionSpec as P

MESH = pl.DeviceIdType.MESH
F32, BF16 = jnp.float32, jnp.bfloat16
DENSE_BYTES = 16 * 2**20
NT = (((1,), (1,)), ((), ()))
NN = (((1,), (0,)), ((), ()))


def split(x):
    high = x.astype(BF16)
    return high, (x - high.astype(F32)).astype(BF16)


def dot_split(stacked, high, b_high, b_low, dims):
    rows = high.shape[0]
    both = lax.dot_general(stacked, b_high, dims, preferred_element_type=F32)
    cross = lax.dot_general(high, b_low, dims, preferred_element_type=F32)
    return both[:rows] + both[rows:] + cross


def product(a, b, dims):
    a_high, a_low = split(a)
    return dot_split(jnp.concatenate([a_high, a_low], 0), a_high, *split(b), dims)


def dense_kernel(row_ref, col_ref, kind_ref, count_ref, values, high_ref, low_ref, held, total, sems):
    step = pl.program_id(0)
    edge = held.shape[1]
    col_tiles = pl.num_programs(0) * (high_ref.shape[3] // edge)

    @pl.when(step == 0)
    def _():
        parts = sems.shape[0]
        size = held.shape[0] // parts
        copies = [
            pltpu.make_async_copy(
                values.at[pl.ds(k * size, size)], held.at[pl.ds(k * size, size)], sems.at[k]
            )
            for k in range(parts)
        ]
        for copy in copies:
            copy.start()

        @pl.loop(0, total.shape[0])
        def _(place):
            total[place] = jnp.zeros(total.shape[1:], F32)

        for copy in copies:
            copy.wait()

        def add(slot, carry):
            place = row_ref[slot] * col_tiles + col_ref[slot]
            total[place] = total[place] + held[kind_ref[slot]]
            return carry

        lax.fori_loop(0, count_ref[0], add, 0)

    _, halves, rows, cols = high_ref.shape
    for half in range(halves):
        for i in range(rows // edge):
            for j in range(cols // edge):
                tile_row = half * (rows // edge) + i
                tile = total[tile_row * col_tiles + step * (cols // edge) + j]
                high, low = split(tile)
                spot = (0, half, pl.ds(i * edge, edge), pl.ds(j * edge, edge))
                high_ref[spot] = high
                low_ref[spot] = low


def dense_blocks(n_row, n_col, stretch, tile_values, tile_row, tile_col, tile_kind, tile_count):
    slots, edge, _ = tile_values.shape
    parts = 8 if slots % 8 == 0 else 1
    shape = jax.ShapeDtypeStruct((n_row, n_col, stretch, stretch), BF16)
    block = pl.BlockSpec((1, n_col, stretch, stretch), lambda i: (i, 0, 0, 0))
    scalars = pl.BlockSpec(memory_space=pltpu.SMEM)
    tiles = (n_row * stretch // edge) * (n_col * stretch // edge)
    return pl.pallas_call(
        dense_kernel,
        grid=(n_row,),
        out_shape=(shape, shape),
        in_specs=[scalars] * 4 + [pl.BlockSpec(memory_space=pl.ANY)],
        out_specs=(block, block),
        scratch_shapes=[
            pltpu.VMEM(tile_values.shape, F32),
            pltpu.VMEM((tiles, edge, edge), F32),
            pltpu.SemaphoreType.DMA((parts,)),
        ],
        compiler_params=pltpu.CompilerParams(vmem_limit_bytes=48 * 2**20),
    )(tile_row, tile_col, tile_kind, tile_count, tile_values)


def layer_kernel(
    n_row, n_col, n_rep, features, weight, cotangent, high_hbm, low_hbm,
    output, input_grad, weight_grad,
    a_high, a_low, xg, cg, yg, part, part_in, pre, hg, z_own, z_sib, z_far, w_own, w_in, w_all,
    a_sem, x_send, x_recv, c_send, c_recv, y_send, y_recv, p_send, p_recv, h_send, h_recv,
    s_send, s_recv, f_send, f_recv, w_send, w_recv, v_send, v_recv,
):
    row, col, rep = lax.axis_index("row"), lax.axis_index("col"), lax.axis_index("rep")
    n_y = n_row // 2
    core, y = lax.rem(row, 2), lax.div(row, 2)
    sibling = y * 2 + (1 - core)
    quarter, stretch = features.shape
    peers = n_row * n_col
    me = row * n_col + col

    def peer(k):
        other = lax.rem(me + k, peers)
        return other, {"row": lax.div(other, n_col), "col": lax.rem(other, n_col)}

    def far(k):
        return lax.rem(y + k, n_y)

    def send(src, dst, send_sem, recv_sem, device):
        return pltpu.make_async_remote_copy(
            src_ref=src, dst_ref=dst, send_sem=send_sem, recv_sem=recv_sem,
            device_id=device, device_id_type=MESH,
        )

    loads = []
    for k in range(n_row):
        origin = (row, sibling)[k] if k < 2 else far(k // 2) * 2 + (core, 1 - core)[k % 2]
        loads.append(origin)
        pltpu.make_async_copy(high_hbm.at[origin], a_high.at[origin], a_sem.at[0, origin]).start()
        pltpu.make_async_copy(low_hbm.at[origin], a_low.at[origin], a_sem.at[1, origin]).start()

    barrier = pltpu.get_barrier_semaphore()
    for k in range(1, peers):
        pl.semaphore_signal(barrier, inc=1, device_id=peer(k)[1], device_id_type=MESH)

    @pl.when(rep > 0)
    def _():
        pl.semaphore_signal(barrier, inc=1, device_id={"rep": rep - 1}, device_id_type=MESH)

    @pl.when(rep < n_rep - 1)
    def _():
        pl.semaphore_signal(barrier, inc=1, device_id={"rep": rep + 1}, device_id_type=MESH)

    ends = jnp.where(rep == 0, 1, 0) + jnp.where(rep == n_rep - 1, 1, 0)
    pl.semaphore_wait(barrier, peers + 1 - ends)

    sent = []

    def start(*args):
        copy = send(*args)
        copy.start()
        sent.append(copy)

    def line_send(buf, send_sem, recv_sem, gap, side, begin):
        origin = rep - gap * side
        go = (origin >= 0) & (origin < n_rep) & (rep + side >= 0) & (rep + side < n_rep)

        @pl.when(go)
        def _():
            copy = send(
                buf.at[origin], buf.at[origin], send_sem.at[(side + 1) // 2, gap],
                recv_sem.at[origin], {"rep": rep + side},
            )
            if begin:
                copy.start()
            else:
                copy.wait_send()

    def line_step(buf, send_sem, recv_sem, gap):
        for side in (1, -1):
            if gap:
                origin = rep - gap * side

                @pl.when((origin >= 0) & (origin < n_rep))
                def _():
                    send(
                        buf.at[origin], buf.at[origin], send_sem.at[0, 0],
                        recv_sem.at[origin], {"rep": rep - side},
                    ).wait_recv()

            if gap < n_rep - 1:
                line_send(buf, send_sem, recv_sem, gap, side, True)

    def arrived(buf, recv_sem, device):
        send(buf, buf, x_send.at[0], recv_sem, device).wait_recv()

    for k in range(1, n_y):
        start(features, xg.at[row], x_send.at[k], x_recv.at[row], {"row": far(k) * 2 + core})
    start(features, xg.at[row], x_send.at[0], x_recv.at[row], {"row": sibling})
    cg[rep] = cotangent[...]
    line_step(cg, c_send, c_recv, 0)
    xg[row] = features[...]

    def forward(origin, first, last):
        for half in (a_high, a_low):
            which = 0 if half is a_high else 1
            hbm = (high_hbm, low_hbm)[which]
            pltpu.make_async_copy(hbm.at[origin], half.at[origin], a_sem.at[which, origin]).wait()
        high, low = split(xg[origin])
        stacked = jnp.concatenate([high, low], 0)
        for k in range(1, n_col + 1):
            dest = lax.rem(col + k, n_col)
            term = dot_split(stacked, high, a_high[origin, dest], a_low[origin, dest], NT)
            part[dest] = term if first else part[dest] + term
            if last and k < n_col:
                start(part.at[dest], part_in.at[col], p_send.at[k], p_recv.at[col], {"col": dest})

    forward(row, True, n_row == 1)
    arrived(xg.at[sibling], x_recv.at[sibling], {"row": sibling})
    forward(sibling, False, n_row == 2)
    for k in range(1, n_y):
        origin = far(k) * 2 + core
        arrived(xg.at[origin], x_recv.at[origin], {"row": origin})
        start(
            xg.at[origin], xg.at[origin], x_send.at[n_y + k - 1], x_recv.at[origin],
            {"row": sibling},
        )
        if k == 1:
            line_step(cg, c_send, c_recv, 1)
        forward(origin, False, False)
        crossed = far(k) * 2 + (1 - core)
        arrived(xg.at[crossed], x_recv.at[crossed], {"row": sibling})
        forward(crossed, False, k == n_y - 1)
    for gap in range(1 if n_y == 1 else 2, n_rep):
        line_step(cg, c_send, c_recv, gap)

    summed = part[col]
    for k in range(1, n_col):
        other = lax.rem(col + k, n_col)
        arrived(part_in.at[other], p_recv.at[other], {"col": other})
        summed = summed + part_in[other]
    yg[rep] = summed
    line_step(yg, y_send, y_recv, 0)
    turned = weight[...].T
    for gap in range(1, n_rep):
        line_step(yg, y_send, y_recv, gap)

    pre[...] = product(turned, yg[...].reshape(n_rep * quarter, stretch), NN)
    scale = (2.0 / 3.141592653589793) ** 0.5

    def bend(v):
        return jnp.tanh(scale * (v + 0.044715 * (v * v * v)))

    v = pre[...]
    t = bend(v)
    slope = 0.5 * (1.0 + t) + 0.5 * v * (1.0 - t * t) * (scale * (1.0 + 0.134145 * (v * v)))
    grad_pre = cg[...].reshape(n_rep * quarter, stretch) * slope
    g_high, g_low = split(grad_pre)
    own = weight[pl.ds(pl.multiple_of(rep * quarter, quarter), quarter), :]
    o_high, o_low = split(own)
    hg[col] = dot_split(jnp.concatenate([o_high, o_low], 0), o_high, g_high, g_low, NN)
    for k in range(1, n_col):
        other = lax.rem(col + k, n_col)
        start(hg.at[col], hg.at[col], h_send.at[k], h_recv.at[col], {"col": other})

    y_high, y_low = split(yg[rep])
    w_part = dot_split(jnp.concatenate([y_high, y_low], 0), y_high, g_high, g_low, NT)
    w_own[...] = w_part.reshape(w_own.shape)
    for k in range(1, peers):
        other, device = peer(k)
        start(w_own.at[other], w_in.at[me], w_send.at[k], w_recv.at[me], device)
    mine = pre[pl.ds(pl.multiple_of(rep * quarter, quarter), quarter), :]
    output[...] = 0.5 * mine * (1.0 + bend(mine))

    def back(k, dest):
        source = lax.rem(col + k, n_col)
        high, low = split(hg[source])
        term = dot_split(
            jnp.concatenate([high, low], 0), high, a_high[dest, source], a_low[dest, source], NN
        )
        z_own[dest] = z_own[dest] + term if k else term

    order = [far(k) * 2 + (1 - core) for k in range(1, n_y)] + [sibling]
    order += [far(k) * 2 + core for k in range(1, n_y)] + [row]
    for dest in order:
        back(0, dest)
    for k in range(1, n_col):
        other = lax.rem(col + k, n_col)
        arrived(hg.at[other], h_recv.at[other], {"col": other})
        for place, dest in enumerate(order):
            back(k, dest)
            if k == n_col - 1:
                ahead = place % n_y + 1
                spot = far(ahead)
                if place < n_y:
                    start(
                        z_own.at[dest], z_sib.at[spot], s_send.at[place], s_recv.at[spot],
                        {"row": sibling},
                    )
                elif place < n_row - 1:
                    arrived(z_sib.at[spot], s_recv.at[spot], {"row": sibling})
                    z_own[dest] = z_own[dest] + z_sib[spot]
                    start(
                        z_own.at[dest], z_far.at[y], f_send.at[ahead], f_recv.at[y], {"row": dest}
                    )

    w_sum = w_own[me]
    for k in range(1, peers):
        other, device = peer(k)
        arrived(w_in.at[other], w_recv.at[other], device)
        w_sum = w_sum + w_in[other]
    w_all[me] = w_sum * float(stretch * peers) ** (-0.5)
    for k in range(1, peers):
        other, device = peer(k)
        start(w_all.at[me], w_all.at[me], v_send.at[k], v_recv.at[me], device)

    arrived(z_sib.at[y], s_recv.at[y], {"row": sibling})
    total = z_own[row] + z_sib[y]
    for k in range(1, n_y):
        arrived(z_far.at[far(k)], f_recv.at[far(k)], {"row": far(k) * 2 + core})
        total = total + z_far[far(k)]
    input_grad[...] = total
    for k in range(1, peers):
        other, device = peer(k)
        arrived(w_all.at[other], v_recv.at[other], device)
    weight_grad[...] = w_all[...].reshape(weight_grad.shape)

    for copy in sent:
        copy.wait_send()
    for gap in range(n_rep - 1):
        for side in (1, -1):
            line_send(cg, c_send, c_recv, gap, side, False)
            line_send(yg, y_send, y_recv, gap, side, False)


def fused(n_row, n_col, n_rep, features, weight, cotangent, tile_values, *slots):
    quarter, stretch = features.shape
    width = weight.shape[0]
    peers = n_row * n_col
    high, low = dense_blocks(n_row, n_col, stretch, tile_values, *slots)
    block = (quarter, stretch)
    vmem = pl.BlockSpec(memory_space=pltpu.VMEM)
    dma = pltpu.SemaphoreType.DMA
    piece = (peers, quarter // peers, width)
    n_y = n_row // 2
    return pl.pallas_call(
        functools.partial(layer_kernel, n_row, n_col, n_rep),
        out_shape=(
            jax.ShapeDtypeStruct(block, F32),
            jax.ShapeDtypeStruct(block, F32),
            jax.ShapeDtypeStruct((quarter, width), F32),
        ),
        in_specs=[vmem] * 3 + [pl.BlockSpec(memory_space=pl.ANY)] * 2,
        out_specs=(vmem,) * 3,
        scratch_shapes=[
            pltpu.VMEM(high.shape, BF16),
            pltpu.VMEM(low.shape, BF16),
            pltpu.VMEM((n_row, *block), F32),
            pltpu.VMEM((n_rep, *block), F32),
            pltpu.VMEM((n_rep, *block), F32),
            pltpu.VMEM((n_col, *block), F32),
            pltpu.VMEM((n_col, *block), F32),
            pltpu.VMEM((n_rep * quarter, stretch), F32),
            pltpu.VMEM((n_col, *block), F32),
            pltpu.VMEM((n_row, *block), F32),
            pltpu.VMEM((n_y, *block), F32),
            pltpu.VMEM((n_y, *block), F32),
            pltpu.VMEM(piece, F32),
            pltpu.VMEM(piece, F32),
            pltpu.VMEM(piece, F32),
            dma((2, n_row)),
            dma((n_row,)), dma((n_row,)),
            dma((2, n_rep)), dma((n_rep,)),
            dma((2, n_rep)), dma((n_rep,)),
            dma((n_col,)), dma((n_col,)),
            dma((n_col,)), dma((n_col,)),
            dma((n_y,)), dma((n_y,)),
            dma((n_y,)), dma((n_y,)),
            dma((peers,)), dma((peers,)),
            dma((peers,)), dma((peers,)),
        ],
        compiler_params=pltpu.CompilerParams(
            collective_id=0, has_side_effects=True, vmem_limit_bytes=48 * 2**20
        ),
    )(features, weight, cotangent, high, low)


def tile_terms(source, values, from_tile, to_tile, tile_kinds, live_weight, dest_tiles, transposed):
    feat_width = source.shape[0]
    tile_edge = values.shape[1]
    tiled = source.reshape(feat_width, source.shape[1] // tile_edge, tile_edge)
    picked = jnp.take(tiled, from_tile, axis=1)
    chosen = jnp.take(values, tile_kinds, axis=0)
    if transposed:
        products = jnp.einsum("fga,gab->fgb", picked, chosen, precision=lax.Precision.HIGHEST)
    else:
        products = jnp.einsum("fgb,gab->fga", picked, chosen, precision=lax.Precision.HIGHEST)
    onehot = (to_tile[:, None] == jnp.arange(dest_tiles, dtype=jnp.int32)[None, :]).astype(
        jnp.float32
    )
    onehot = onehot * live_weight[:, None]
    spread = jnp.einsum("fgt,gd->fdt", products, onehot, precision=lax.Precision.HIGHEST)
    return spread.reshape(feat_width, dest_tiles * tile_edge)


def aggregate(source, values, from_tile, to_tile, tile_kinds, live_count, dest_tiles, transposed):
    slot_total = tile_kinds.shape[0]
    live_weight = (jnp.arange(slot_total, dtype=jnp.int32) < live_count).astype(jnp.float32)
    return tile_terms(
        source, values, from_tile, to_tile, tile_kinds, live_weight, dest_tiles, transposed
    )


def local(features, weight, cotangent, tile_values, tile_row, tile_col, tile_kind, tile_count):
    n_rowdev = lax.axis_size("row")
    n_coldev = lax.axis_size("col")
    n_repdev = lax.axis_size("rep")
    quarter, stretch_len = features.shape
    nodes = n_rowdev * n_coldev
    if (
        n_rowdev * n_coldev * stretch_len * stretch_len * 4 <= DENSE_BYTES
        and n_rowdev % 2 == 0
        and n_coldev > 1
        and n_repdev > 1
        and quarter % (8 * nodes) == 0
    ):
        return fused(
            n_rowdev, n_coldev, n_repdev, features, weight, cotangent, tile_values,
            tile_row, tile_col, tile_kind, tile_count,
        )
    own_rows = lax.dynamic_slice_in_dim(weight, lax.axis_index("rep") * quarter, quarter, 0)
    tile_edge = tile_values.shape[1]
    live_count = tile_count[0]
    row_tiles = n_coldev * stretch_len // tile_edge
    col_tiles = n_rowdev * stretch_len // tile_edge
    mixed = lax.psum_scatter(
        lax.dot_general(
            own_rows,
            features,
            (((0,), (0,)), ((), ())),
            precision=lax.Precision.HIGHEST,
            preferred_element_type=jnp.float32,
        ),
        "rep",
        scatter_dimension=0,
        tiled=True,
    )
    column_block = lax.all_gather(mixed, "row", axis=1, tiled=True)
    partial_value = aggregate(
        column_block, tile_values, tile_col, tile_row, tile_kind, live_count, row_tiles, False
    )
    summed = lax.psum_scatter(partial_value, "col", scatter_dimension=1, tiled=True)
    output, pullback = jax.vjp(lambda v: jax.nn.gelu(v, approximate=True), summed)
    (grad_pre,) = pullback(cotangent)
    row_block = lax.all_gather(grad_pre, "col", axis=1, tiled=True)
    partial_back = aggregate(
        row_block, tile_values, tile_row, tile_col, tile_kind, live_count, col_tiles, True
    )
    grad_mixed = lax.psum_scatter(partial_back, "row", scatter_dimension=1, tiled=True)
    whole = lax.all_gather(grad_mixed, "rep", axis=0, tiled=True)
    input_grad = jnp.dot(
        own_rows, whole, preferred_element_type=jnp.float32, precision=lax.Precision.HIGHEST
    )
    weight_part = lax.dot_general(
        features,
        whole,
        (((1,), (1,)), ((), ())),
        precision=lax.Precision.HIGHEST,
        preferred_element_type=jnp.float32,
    )
    node_total = stretch_len * n_rowdev * n_coldev
    weight_grad = lax.psum(weight_part * float(node_total) ** (-0.5), ("row", "col"))
    return (output, input_grad, weight_grad)


def solution(mesh):
    return jax.shard_map(
        local,
        mesh=mesh,
        in_specs=(
            P("rep", ("col", "row")),
            P(),
            P("rep", ("row", "col")),
            P(("row", "col"), None, None),
            P(("row", "col")),
            P(("row", "col")),
            P(("row", "col")),
            P(("row", "col")),
        ),
        out_specs=(P("rep", ("row", "col")), P("rep", ("col", "row")), P("rep", None)),
        check_vma=False,
    )
```

```python
import functools

import jax
import jax.numpy as jnp
from jax import lax
from jax.experimental import pallas as pl
from jax.experimental.pallas import tpu as pltpu
from jax.sharding import PartitionSpec as P

MESH = pl.DeviceIdType.MESH
F32, BF16 = jnp.float32, jnp.bfloat16
DENSE_BYTES = 16 * 2**20
NT = (((1,), (1,)), ((), ()))
NN = (((1,), (0,)), ((), ()))


def split(x):
    high = x.astype(BF16)
    return high, (x - high.astype(F32)).astype(BF16)


def dot_split(stacked, high, b_high, b_low, dims):
    rows = high.shape[0]
    both = lax.dot_general(stacked, b_high, dims, preferred_element_type=F32)
    cross = lax.dot_general(high, b_low, dims, preferred_element_type=F32)
    return both[:rows] + both[rows:] + cross


def product(a, b, dims):
    a_high, a_low = split(a)
    return dot_split(jnp.concatenate([a_high, a_low], 0), a_high, *split(b), dims)


def chain_links(row_tiles, col_tiles, count, tile_row, tile_col):
    slots = tile_row.shape[1]
    queries = slots + row_tiles * col_tiles
    place = tile_row * col_tiles + tile_col
    shape = (slots, slots)
    key, query = (lax.broadcasted_iota(jnp.int32, shape, axis) for axis in (0, 1))
    keys = jnp.max(jnp.where(key == query, place, 0), axis=1, keepdims=True)

    def latest(hit, key):
        last = jnp.max(jnp.where(hit & (key < count), key, -1), axis=0, keepdims=True)
        return jnp.where(last < 0, slots, last)

    before = latest((keys == place) & (key < query), key)
    shape = (slots, row_tiles * col_tiles)
    key, query = (lax.broadcasted_iota(jnp.int32, shape, axis) for axis in (0, 1))
    return before, latest(keys == query, key)


def layer_kernel(
    n_row, n_col, n_rep, kind, count, tile_row, tile_col, features_in, weight_in, cotangent_in, values_in,
    output, input_grad, weight_grad,
    before_v, last_v, before, last, held, chain, weight, a_high, a_low, xs, xg, cg, yg, part, part_in, pre, hg, z_own, z_sib, z_far, w_own, w_in, w_all,
    l_sem, i_sem, t_sem, x_send, x_recv, c_send, c_recv, y_send, y_recv, p_send, p_recv, h_send, h_recv,
    s_send, s_recv, f_send, f_recv, w_send, w_recv, v_send, v_recv,
):
    row, col, rep = lax.axis_index("row"), lax.axis_index("col"), lax.axis_index("rep")
    n_y = n_row // 2
    core, y = lax.rem(row, 2), lax.div(row, 2)
    sibling = y * 2 + (1 - core)
    quarter, stretch = features_in.shape
    slots, edge, _ = held.shape
    tiles = stretch // edge
    peers = n_row * n_col
    me = row * n_col + col

    def peer(k):
        other = lax.rem(me + k, peers)
        return other, {"row": lax.div(other, n_col), "col": lax.rem(other, n_col)}

    def far(k):
        return lax.rem(y + k, n_y)

    def send(src, dst, send_sem, recv_sem, device):
        return pltpu.make_async_remote_copy(
            src_ref=src, dst_ref=dst, send_sem=send_sem, recv_sem=recv_sem,
            device_id=device, device_id_type=MESH,
        )

    inputs = [
        pltpu.make_async_copy(features_in, xg.at[row], i_sem.at[0]),
        pltpu.make_async_copy(cotangent_in, cg.at[rep], i_sem.at[1]),
        pltpu.make_async_copy(weight_in, weight, i_sem.at[2]),
    ]
    parts = t_sem.shape[0]
    size = slots // parts
    for k in range(parts):
        piece = pl.ds(k * size, size)
        inputs.append(pltpu.make_async_copy(values_in.at[piece], held.at[piece], t_sem.at[k]))
    for copy in inputs:
        copy.start()

    links = chain_links(
        n_col * tiles, n_row * tiles, count[0],
        tile_row[...].reshape(1, slots), tile_col[...].reshape(1, slots),
    )
    before_v[...], last_v[...] = links
    moves = [
        pltpu.make_async_copy(before_v, before, l_sem.at[0]),
        pltpu.make_async_copy(last_v, last, l_sem.at[1]),
    ]
    for copy in moves:
        copy.start()

    barrier = pltpu.get_barrier_semaphore()
    for k in range(1, peers):
        pl.semaphore_signal(barrier, inc=1, device_id=peer(k)[1], device_id_type=MESH)

    @pl.when(rep > 0)
    def _():
        pl.semaphore_signal(barrier, inc=1, device_id={"rep": rep - 1}, device_id_type=MESH)

    @pl.when(rep < n_rep - 1)
    def _():
        pl.semaphore_signal(barrier, inc=1, device_id={"rep": rep + 1}, device_id_type=MESH)

    ends = jnp.where(rep == 0, 1, 0) + jnp.where(rep == n_rep - 1, 1, 0)
    pl.semaphore_wait(barrier, peers + 1 - ends)

    sent = []

    def start(*args):
        copy = send(*args)
        copy.start()
        sent.append(copy)

    def line_send(buf, send_sem, recv_sem, gap, side, begin):
        origin = rep - gap * side
        go = (origin >= 0) & (origin < n_rep) & (rep + side >= 0) & (rep + side < n_rep)

        @pl.when(go)
        def _():
            copy = send(
                buf.at[origin], buf.at[origin], send_sem.at[(side + 1) // 2, gap],
                recv_sem.at[origin], {"rep": rep + side},
            )
            if begin:
                copy.start()
            else:
                copy.wait_send()

    def line_step(buf, send_sem, recv_sem, gap):
        for side in (1, -1):
            if gap:
                origin = rep - gap * side

                @pl.when((origin >= 0) & (origin < n_rep))
                def _():
                    send(
                        buf.at[origin], buf.at[origin], send_sem.at[0, 0],
                        recv_sem.at[origin], {"rep": rep - side},
                    ).wait_recv()

            if gap < n_rep - 1:
                line_send(buf, send_sem, recv_sem, gap, side, True)

    def arrived(buf, recv_sem, device):
        send(buf, buf, x_send.at[0], recv_sem, device).wait_recv()

    inputs[0].wait()
    for k in range(1, n_y):
        start(xg.at[row], xg.at[row], x_send.at[k], x_recv.at[row], {"row": far(k) * 2 + core})
    start(xg.at[row], xg.at[row], x_send.at[0], x_recv.at[row], {"row": sibling})
    inputs[1].wait()
    line_step(cg, c_send, c_recv, 0)

    for copy in inputs[2:] + moves:
        copy.wait()
    chain[slots] = jnp.zeros((edge, edge), F32)

    @pl.loop(0, slots, unroll=4 if slots % 4 == 0 else 1)
    def _(slot):
        chain[slot] = held[kind[slot]] + chain[before[0, slot]]

    def ready(origin):
        high, low = split(xg[origin])
        xs[origin, :quarter, :] = high
        xs[origin, quarter:, :] = low

    ready(row)
    for k in range(1, n_y):
        origin = far(k) * 2 + core
        arrived(xg.at[origin], x_recv.at[origin], {"row": origin})
        start(
            xg.at[origin], xg.at[origin], x_send.at[n_y + k - 1], x_recv.at[origin],
            {"row": sibling},
        )
        ready(origin)
    arrived(xg.at[sibling], x_recv.at[sibling], {"row": sibling})
    ready(sibling)
    line_step(cg, c_send, c_recv, 1)

    def dense(origin, dest):
        @pl.loop(0, tiles)
        def _(i):
            for j in range(tiles):
                place = ((dest * tiles + i) * n_row + origin) * tiles + j
                high, low = split(chain[last[0, place]])
                rows = pl.ds(pl.multiple_of(i * edge, edge), edge)
                a_high[origin, dest, rows, pl.ds(j * edge, edge)] = high
                a_low[origin, dest, rows, pl.ds(j * edge, edge)] = low

    for k in range(1, n_col + 1):
        dest = lax.rem(col + k, n_col)
        for place in range(n_row):
            if place < n_y:
                origin = far(place) * 2 + core
            else:
                origin = far(place - n_y) * 2 + (1 - core)
            if k == 1 and place > n_y:
                arrived(xg.at[origin], x_recv.at[origin], {"row": sibling})
                ready(origin)
            dense(origin, dest)
            stacked = xs[origin]
            term = dot_split(
                stacked, stacked[:quarter], a_high[origin, dest], a_low[origin, dest], NT
            )
            part[dest] = part[dest] + term if place else term
        if k < n_col:
            start(part.at[dest], part_in.at[col], p_send.at[k], p_recv.at[col], {"col": dest})
        if k == 1:
            for gap in range(2, n_rep):
                line_step(cg, c_send, c_recv, gap)

    summed = part[col]
    for k in range(1, n_col):
        other = lax.rem(col + k, n_col)
        arrived(part_in.at[other], p_recv.at[other], {"col": other})
        summed = summed + part_in[other]
    yg[rep] = summed
    line_step(yg, y_send, y_recv, 0)
    turned = weight[...].T
    for gap in range(1, n_rep):
        line_step(yg, y_send, y_recv, gap)

    pre[...] = product(turned, yg[...].reshape(n_rep * quarter, stretch), NN)
    scale = (2.0 / 3.141592653589793) ** 0.5

    def bend(v):
        return jnp.tanh(scale * (v + 0.044715 * (v * v * v)))

    v = pre[...]
    t = bend(v)
    slope = 0.5 * (1.0 + t) + 0.5 * v * (1.0 - t * t) * (scale * (1.0 + 0.134145 * (v * v)))
    grad_pre = cg[...].reshape(n_rep * quarter, stretch) * slope
    g_high, g_low = split(grad_pre)
    own = weight[pl.ds(pl.multiple_of(rep * quarter, quarter), quarter), :]
    o_high, o_low = split(own)
    hg[col] = dot_split(jnp.concatenate([o_high, o_low], 0), o_high, g_high, g_low, NN)
    for k in range(1, n_col):
        other = lax.rem(col + k, n_col)
        start(hg.at[col], hg.at[col], h_send.at[k], h_recv.at[col], {"col": other})

    y_high, y_low = split(yg[rep])
    w_part = dot_split(jnp.concatenate([y_high, y_low], 0), y_high, g_high, g_low, NT)
    w_own[...] = w_part.reshape(w_own.shape)
    for k in range(1, peers):
        other, device = peer(k)
        start(w_own.at[other], w_in.at[me], w_send.at[k], w_recv.at[me], device)
    mine = pre[pl.ds(pl.multiple_of(rep * quarter, quarter), quarter), :]
    output[...] = 0.5 * mine * (1.0 + bend(mine))

    def back(k, dest):
        source = lax.rem(col + k, n_col)
        high, low = split(hg[source])
        term = dot_split(
            jnp.concatenate([high, low], 0), high, a_high[dest, source], a_low[dest, source], NN
        )
        z_own[dest] = z_own[dest] + term if k else term

    order = [far(k) * 2 + (1 - core) for k in range(1, n_y)] + [sibling]
    order += [far(k) * 2 + core for k in range(1, n_y)] + [row]
    for dest in order:
        back(0, dest)
    for k in range(1, n_col):
        other = lax.rem(col + k, n_col)
        arrived(hg.at[other], h_recv.at[other], {"col": other})
        for place, dest in enumerate(order):
            back(k, dest)
            if k == n_col - 1:
                ahead = place % n_y + 1
                spot = far(ahead)
                if place < n_y:
                    start(
                        z_own.at[dest], z_sib.at[spot], s_send.at[place], s_recv.at[spot],
                        {"row": sibling},
                    )
                elif place < n_row - 1:
                    arrived(z_sib.at[spot], s_recv.at[spot], {"row": sibling})
                    z_own[dest] = z_own[dest] + z_sib[spot]
                    start(
                        z_own.at[dest], z_far.at[y], f_send.at[ahead], f_recv.at[y], {"row": dest}
                    )

    w_sum = w_own[me]
    for k in range(1, peers):
        other, device = peer(k)
        arrived(w_in.at[other], w_recv.at[other], device)
        w_sum = w_sum + w_in[other]
    w_all[me] = w_sum * float(stretch * peers) ** (-0.5)
    for k in range(1, peers):
        other, device = peer(k)
        start(w_all.at[me], w_all.at[me], v_send.at[k], v_recv.at[me], device)

    arrived(z_sib.at[y], s_recv.at[y], {"row": sibling})
    total = z_own[row] + z_sib[y]
    for k in range(1, n_y):
        arrived(z_far.at[far(k)], f_recv.at[far(k)], {"row": far(k) * 2 + core})
        total = total + z_far[far(k)]
    input_grad[...] = total
    for k in range(1, peers):
        other, device = peer(k)
        arrived(w_all.at[other], v_recv.at[other], device)
    weight_grad[...] = w_all[...].reshape(weight_grad.shape)

    for copy in sent:
        copy.wait_send()
    for gap in range(n_rep - 1):
        for side in (1, -1):
            line_send(cg, c_send, c_recv, gap, side, False)
            line_send(yg, y_send, y_recv, gap, side, False)


def fused(
    n_row, n_col, n_rep, features, weight, cotangent, tile_values, tile_row, tile_col, tile_kind,
    tile_count,
):
    quarter, stretch = features.shape
    width = weight.shape[0]
    peers = n_row * n_col
    slots, edge, _ = tile_values.shape
    row_tiles, col_tiles = n_col * stretch // edge, n_row * stretch // edge
    parts = 8 if slots % 8 == 0 else 1
    dense = (n_row, n_col, stretch, stretch)
    block = (quarter, stretch)
    vmem = pl.BlockSpec(memory_space=pltpu.VMEM)
    smem = pl.BlockSpec(memory_space=pltpu.SMEM)
    dma = pltpu.SemaphoreType.DMA
    piece = (peers, quarter // peers, width)
    n_y = n_row // 2
    return pl.pallas_call(
        functools.partial(layer_kernel, n_row, n_col, n_rep),
        out_shape=(
            jax.ShapeDtypeStruct(block, F32),
            jax.ShapeDtypeStruct(block, F32),
            jax.ShapeDtypeStruct((quarter, width), F32),
        ),
        in_specs=[smem] * 2 + [vmem] * 2 + [pl.BlockSpec(memory_space=pl.ANY)] * 4,
        out_specs=(vmem,) * 3,
        scratch_shapes=[
            pltpu.VMEM((1, slots), jnp.int32),
            pltpu.VMEM((1, row_tiles * col_tiles), jnp.int32),
            pltpu.SMEM((1, slots), jnp.int32),
            pltpu.SMEM((1, row_tiles * col_tiles), jnp.int32),
            pltpu.VMEM(tile_values.shape, F32),
            pltpu.VMEM((slots + 1, edge, edge), F32),
            pltpu.VMEM(weight.shape, F32),
            pltpu.VMEM(dense, BF16),
            pltpu.VMEM(dense, BF16),
            pltpu.VMEM((n_row, 2 * quarter, stretch), BF16),
            pltpu.VMEM((n_row, *block), F32),
            pltpu.VMEM((n_rep, *block), F32),
            pltpu.VMEM((n_rep, *block), F32),
            pltpu.VMEM((n_col, *block), F32),
            pltpu.VMEM((n_col, *block), F32),
            pltpu.VMEM((n_rep * quarter, stretch), F32),
            pltpu.VMEM((n_col, *block), F32),
            pltpu.VMEM((n_row, *block), F32),
            pltpu.VMEM((n_y, *block), F32),
            pltpu.VMEM((n_y, *block), F32),
            pltpu.VMEM(piece, F32),
            pltpu.VMEM(piece, F32),
            pltpu.VMEM(piece, F32),
            dma((2,)), dma((3,)), dma((parts,)),
            dma((n_row,)), dma((n_row,)),
            dma((2, n_rep)), dma((n_rep,)),
            dma((2, n_rep)), dma((n_rep,)),
            dma((n_col,)), dma((n_col,)),
            dma((n_col,)), dma((n_col,)),
            dma((n_y,)), dma((n_y,)),
            dma((n_y,)), dma((n_y,)),
            dma((peers,)), dma((peers,)),
            dma((peers,)), dma((peers,)),
        ],
        compiler_params=pltpu.CompilerParams(
            collective_id=0, has_side_effects=True, vmem_limit_bytes=56 * 2**20
        ),
    )(tile_kind, tile_count, tile_row, tile_col, features, weight, cotangent, tile_values)


def tile_terms(source, values, from_tile, to_tile, tile_kinds, live_weight, dest_tiles, transposed):
    feat_width = source.shape[0]
    tile_edge = values.shape[1]
    tiled = source.reshape(feat_width, source.shape[1] // tile_edge, tile_edge)
    picked = jnp.take(tiled, from_tile, axis=1)
    chosen = jnp.take(values, tile_kinds, axis=0)
    if transposed:
        products = jnp.einsum("fga,gab->fgb", picked, chosen, precision=lax.Precision.HIGHEST)
    else:
        products = jnp.einsum("fgb,gab->fga", picked, chosen, precision=lax.Precision.HIGHEST)
    onehot = (to_tile[:, None] == jnp.arange(dest_tiles, dtype=jnp.int32)[None, :]).astype(
        jnp.float32
    )
    onehot = onehot * live_weight[:, None]
    spread = jnp.einsum("fgt,gd->fdt", products, onehot, precision=lax.Precision.HIGHEST)
    return spread.reshape(feat_width, dest_tiles * tile_edge)


def aggregate(source, values, from_tile, to_tile, tile_kinds, live_count, dest_tiles, transposed):
    slot_total = tile_kinds.shape[0]
    live_weight = (jnp.arange(slot_total, dtype=jnp.int32) < live_count).astype(jnp.float32)
    return tile_terms(
        source, values, from_tile, to_tile, tile_kinds, live_weight, dest_tiles, transposed
    )


def local(features, weight, cotangent, tile_values, tile_row, tile_col, tile_kind, tile_count):
    n_rowdev = lax.axis_size("row")
    n_coldev = lax.axis_size("col")
    n_repdev = lax.axis_size("rep")
    quarter, stretch_len = features.shape
    nodes = n_rowdev * n_coldev
    if (
        n_rowdev * n_coldev * stretch_len * stretch_len * 4 <= DENSE_BYTES
        and n_rowdev % 2 == 0
        and n_coldev > 1
        and n_repdev > 1
        and quarter % (8 * nodes) == 0
        and tile_values.size * 4 <= DENSE_BYTES
    ):
        return fused(
            n_rowdev, n_coldev, n_repdev, features, weight, cotangent, tile_values,
            tile_row, tile_col, tile_kind, tile_count,
        )
    own_rows = lax.dynamic_slice_in_dim(weight, lax.axis_index("rep") * quarter, quarter, 0)
    tile_edge = tile_values.shape[1]
    live_count = tile_count[0]
    row_tiles = n_coldev * stretch_len // tile_edge
    col_tiles = n_rowdev * stretch_len // tile_edge
    mixed = lax.psum_scatter(
        lax.dot_general(
            own_rows,
            features,
            (((0,), (0,)), ((), ())),
            precision=lax.Precision.HIGHEST,
            preferred_element_type=jnp.float32,
        ),
        "rep",
        scatter_dimension=0,
        tiled=True,
    )
    column_block = lax.all_gather(mixed, "row", axis=1, tiled=True)
    partial_value = aggregate(
        column_block, tile_values, tile_col, tile_row, tile_kind, live_count, row_tiles, False
    )
    summed = lax.psum_scatter(partial_value, "col", scatter_dimension=1, tiled=True)
    output, pullback = jax.vjp(lambda v: jax.nn.gelu(v, approximate=True), summed)
    (grad_pre,) = pullback(cotangent)
    row_block = lax.all_gather(grad_pre, "col", axis=1, tiled=True)
    partial_back = aggregate(
        row_block, tile_values, tile_row, tile_col, tile_kind, live_count, col_tiles, True
    )
    grad_mixed = lax.psum_scatter(partial_back, "row", scatter_dimension=1, tiled=True)
    whole = lax.all_gather(grad_mixed, "rep", axis=0, tiled=True)
    input_grad = jnp.dot(
        own_rows, whole, preferred_element_type=jnp.float32, precision=lax.Precision.HIGHEST
    )
    weight_part = lax.dot_general(
        features,
        whole,
        (((1,), (1,)), ((), ())),
        precision=lax.Precision.HIGHEST,
        preferred_element_type=jnp.float32,
    )
    node_total = stretch_len * n_rowdev * n_coldev
    weight_grad = lax.psum(weight_part * float(node_total) ** (-0.5), ("row", "col"))
    return (output, input_grad, weight_grad)


def solution(mesh):
    return jax.shard_map(
        local,
        mesh=mesh,
        in_specs=(
            P("rep", ("col", "row")),
            P(),
            P("rep", ("row", "col")),
            P(("row", "col"), None, None),
            P(("row", "col")),
            P(("row", "col")),
            P(("row", "col")),
            P(("row", "col")),
        ),
        out_specs=(P("rep", ("row", "col")), P("rep", ("col", "row")), P("rep", None)),
        check_vma=False,
    )
```

```python
import functools

import jax
import jax.numpy as jnp
from jax import lax
from jax.experimental import pallas as pl
from jax.experimental.pallas import tpu as pltpu
from jax.sharding import PartitionSpec as P

MESH = pl.DeviceIdType.MESH
F32, BF16 = jnp.float32, jnp.bfloat16
DENSE_BYTES = 16 * 2**20
NT = (((1,), (1,)), ((), ()))
NN = (((1,), (0,)), ((), ()))


def split(x):
    high = x.astype(BF16)
    return high, (x - high.astype(F32)).astype(BF16)


def dot_split(stacked, high, b_high, b_low, dims):
    rows = high.shape[0]
    both = lax.dot_general(stacked, b_high, dims, preferred_element_type=F32)
    cross = lax.dot_general(high, b_low, dims, preferred_element_type=F32)
    return both[:rows] + both[rows:] + cross


def product(a, b, dims):
    a_high, a_low = split(a)
    return dot_split(jnp.concatenate([a_high, a_low], 0), a_high, *split(b), dims)


def chain_links(row_tiles, col_tiles, count, tile_row, tile_col):
    slots = tile_row.shape[1]
    queries = slots + row_tiles * col_tiles
    place = tile_row * col_tiles + tile_col
    shape = (slots, slots)
    key, query = (lax.broadcasted_iota(jnp.int32, shape, axis) for axis in (0, 1))
    keys = jnp.max(jnp.where(key == query, place, 0), axis=1, keepdims=True)

    def latest(hit, key):
        last = jnp.max(jnp.where(hit & (key < count), key, -1), axis=0, keepdims=True)
        return jnp.where(last < 0, slots, last)

    before = latest((keys == place) & (key < query), key)
    shape = (slots, row_tiles * col_tiles)
    key, query = (lax.broadcasted_iota(jnp.int32, shape, axis) for axis in (0, 1))
    return before, latest(keys == query, key)


def layer_kernel(
    n_row, n_col, n_rep, kind, count, tile_row, tile_col, features_in, weight_in, cotangent_in, values_in,
    output, input_grad, weight_grad,
    before_v, last_v, before, last, held, chain, weight, a_high, a_low, xs, xg, cg, yg, part, part_in, pre, hg, z_own, z_sib, z_far, w_own, w_in, w_all,
    l_sem, i_sem, t_sem, x_send, x_recv, c_send, c_recv, y_send, y_recv, p_send, p_recv, h_send, h_recv,
    s_send, s_recv, f_send, f_recv, w_send, w_recv, v_send, v_recv,
):
    row, col, rep = lax.axis_index("row"), lax.axis_index("col"), lax.axis_index("rep")
    n_y = n_row // 2
    core, y = lax.rem(row, 2), lax.div(row, 2)
    sibling = y * 2 + (1 - core)
    quarter, stretch = features_in.shape
    slots, edge, _ = held.shape
    tiles = stretch // edge
    peers = n_row * n_col
    me = row * n_col + col

    def peer(k):
        other = lax.rem(me + k, peers)
        return other, {"row": lax.div(other, n_col), "col": lax.rem(other, n_col)}

    def far(k):
        return lax.rem(y + k, n_y)

    def send(src, dst, send_sem, recv_sem, device):
        return pltpu.make_async_remote_copy(
            src_ref=src, dst_ref=dst, send_sem=send_sem, recv_sem=recv_sem,
            device_id=device, device_id_type=MESH,
        )

    inputs = [
        pltpu.make_async_copy(features_in, xg.at[row], i_sem.at[0]),
        pltpu.make_async_copy(cotangent_in, cg.at[rep, 0], i_sem.at[1]),
        pltpu.make_async_copy(weight_in, weight, i_sem.at[2]),
    ]
    parts = t_sem.shape[0]
    size = slots // parts
    for k in range(parts):
        piece = pl.ds(k * size, size)
        inputs.append(pltpu.make_async_copy(values_in.at[piece], held.at[piece], t_sem.at[k]))
    for copy in inputs:
        copy.start()

    links = chain_links(
        n_col * tiles, n_row * tiles, count[0],
        tile_row[...].reshape(1, slots), tile_col[...].reshape(1, slots),
    )
    before_v[...], last_v[...] = links
    moves = [
        pltpu.make_async_copy(before_v, before, l_sem.at[0]),
        pltpu.make_async_copy(last_v, last, l_sem.at[1]),
    ]
    for copy in moves:
        copy.start()

    barrier = pltpu.get_barrier_semaphore()
    for k in range(1, peers):
        pl.semaphore_signal(barrier, inc=1, device_id=peer(k)[1], device_id_type=MESH)

    @pl.when(rep > 0)
    def _():
        pl.semaphore_signal(barrier, inc=1, device_id={"rep": rep - 1}, device_id_type=MESH)

    @pl.when(rep < n_rep - 1)
    def _():
        pl.semaphore_signal(barrier, inc=1, device_id={"rep": rep + 1}, device_id_type=MESH)

    ends = jnp.where(rep == 0, 1, 0) + jnp.where(rep == n_rep - 1, 1, 0)
    pl.semaphore_wait(barrier, peers + 1 - ends)

    sent = []

    def start(*args):
        copy = send(*args)
        copy.start()
        sent.append(copy)

    def line_send(buf, send_sem, recv_sem, piece, gap, side, begin):
        origin = rep - gap * side
        go = (origin >= 0) & (origin < n_rep) & (rep + side >= 0) & (rep + side < n_rep)

        @pl.when(go)
        def _():
            copy = send(
                buf.at[origin, piece], buf.at[origin, piece],
                send_sem.at[(side + 1) // 2, gap, piece], recv_sem.at[origin, piece],
                {"rep": rep + side},
            )
            if begin:
                copy.start()
            else:
                copy.wait_send()

    def line_step(buf, send_sem, recv_sem, piece, gap):
        for side in (1, -1):
            if gap:
                origin = rep - gap * side

                @pl.when((origin >= 0) & (origin < n_rep))
                def _():
                    send(
                        buf.at[origin, piece], buf.at[origin, piece], send_sem.at[0, 0, 0],
                        recv_sem.at[origin, piece], {"rep": rep - side},
                    ).wait_recv()

            if gap < n_rep - 1:
                line_send(buf, send_sem, recv_sem, piece, gap, side, True)

    def arrived(buf, recv_sem, device):
        send(buf, buf, x_send.at[0], recv_sem, device).wait_recv()

    inputs[0].wait()
    for k in range(1, n_y):
        start(xg.at[row], xg.at[row], x_send.at[k], x_recv.at[row], {"row": far(k) * 2 + core})
    start(xg.at[row], xg.at[row], x_send.at[0], x_recv.at[row], {"row": sibling})
    inputs[1].wait()
    line_step(cg, c_send, c_recv, 0, 0)

    for copy in inputs[2:] + moves:
        copy.wait()
    chain[slots] = jnp.zeros((edge, edge), F32)

    @pl.loop(0, slots, unroll=4 if slots % 4 == 0 else 1)
    def _(slot):
        chain[slot] = held[kind[slot]] + chain[before[0, slot]]

    def ready(origin):
        high, low = split(xg[origin])
        both = jnp.concatenate([high.astype(F32), low.astype(F32)], 0).T
        xs[pl.ds(pl.multiple_of(origin * stretch, stretch), stretch), :] = both.astype(BF16)

    ready(row)
    for k in range(1, n_y):
        origin = far(k) * 2 + core
        arrived(xg.at[origin], x_recv.at[origin], {"row": origin})
        start(
            xg.at[origin], xg.at[origin], x_send.at[n_y + k - 1], x_recv.at[origin],
            {"row": sibling},
        )
        ready(origin)
    arrived(xg.at[sibling], x_recv.at[sibling], {"row": sibling})
    ready(sibling)
    line_step(cg, c_send, c_recv, 0, 1)

    pieces = yg.shape[1]
    short = stretch // pieces
    spans = [pl.ds(piece * short, short) for piece in range(pieces)]

    def dense(dest, piece):
        @pl.loop(0, short // edge)
        def _(i):
            first = (dest * tiles + piece * (short // edge) + i) * (n_row * tiles)
            rows = pl.ds(pl.multiple_of(piece * short + i * edge, edge), edge)
            for j in range(n_row * tiles):
                high, low = split(chain[last[0, first + j]])
                a_high[dest, rows, pl.ds(j * edge, edge)] = high
                a_low[dest, rows, pl.ds(j * edge, edge)] = low

    def aggregate_piece(dest, piece):
        nodes = xs[...]
        term = jnp.dot(a_high[dest, spans[piece], :], nodes, preferred_element_type=F32)
        term += jnp.dot(a_low[dest, spans[piece], :], nodes, preferred_element_type=F32)
        term = term.T
        return term[:quarter] + term[quarter:]

    for k in range(1, n_col):
        dest = lax.rem(col + k, n_col)
        for piece in range(pieces):
            dense(dest, piece)
            if k == 1 and piece == 0:
                for far_y in range(1, n_y):
                    origin = far(far_y) * 2 + (1 - core)
                    arrived(xg.at[origin], x_recv.at[origin], {"row": sibling})
                    ready(origin)
            part[dest, piece] = aggregate_piece(dest, piece)
            start(
                part.at[dest, piece], part_in.at[col, piece], p_send.at[k, piece],
                p_recv.at[col, piece], {"col": dest},
            )
    for gap in range(2, n_rep):
        line_step(cg, c_send, c_recv, 0, gap)

    for piece in range(pieces):
        dense(col, piece)
        summed = aggregate_piece(col, piece)
        for k in range(1, n_col):
            other = lax.rem(col + k, n_col)
            arrived(part_in.at[other, piece], p_recv.at[other, piece], {"col": other})
            summed = summed + part_in[other, piece]
        yg[rep, piece] = summed
        line_step(yg, y_send, y_recv, piece, 0)
    turned = weight[...].T
    t_high, t_low = split(turned)
    t_both = jnp.concatenate([t_high, t_low], 0)
    own = weight[pl.ds(pl.multiple_of(rep * quarter, quarter), quarter), :]
    o_high, o_low = split(own)
    o_both = jnp.concatenate([o_high, o_low], 0)
    scale = (2.0 / 3.141592653589793) ** 0.5

    def bend(v):
        return jnp.tanh(scale * (v + 0.044715 * (v * v * v)))

    for gap in range(1, n_rep - 1):
        for piece in range(pieces):
            line_step(yg, y_send, y_recv, piece, gap)

    w_part = None
    width = n_rep * quarter
    for piece in range(pieces):
        line_step(yg, y_send, y_recv, piece, n_rep - 1)
        gathered = jnp.concatenate([yg[origin, piece] for origin in range(n_rep)], 0)
        v = dot_split(t_both, t_high, *split(gathered), NN)
        pre[:, spans[piece]] = v
        t = bend(v)
        slope = 0.5 * (1.0 + t) + 0.5 * v * (1.0 - t * t) * (scale * (1.0 + 0.134145 * (v * v)))
        grad_pre = cg[:, 0, :, spans[piece]].reshape(width, short) * slope
        g_high, g_low = split(grad_pre)
        hg[col, piece] = dot_split(o_both, o_high, g_high, g_low, NN)
        for k in range(1, n_col):
            other = lax.rem(col + k, n_col)
            start(
                hg.at[col, piece], hg.at[col, piece], h_send.at[k, piece], h_recv.at[col, piece],
                {"col": other},
            )
        y_high, y_low = split(yg[rep, piece])
        term = dot_split(jnp.concatenate([y_high, y_low], 0), y_high, g_high, g_low, NT)
        w_part = term if w_part is None else w_part + term

    w_own[...] = w_part.reshape(w_own.shape)
    for k in range(1, peers):
        other, device = peer(k)
        start(w_own.at[other], w_in.at[me], w_send.at[k], w_recv.at[me], device)
    mine = pre[pl.ds(pl.multiple_of(rep * quarter, quarter), quarter), :]
    output[...] = 0.5 * mine * (1.0 + bend(mine))

    def parts_of(source):
        high, low = split(jnp.concatenate([hg[source, piece] for piece in range(pieces)], 1))
        return jnp.concatenate([high, low], 0), high

    def back(k, dest, stacked, high):
        source = lax.rem(col + k, n_col)
        span = pl.ds(pl.multiple_of(dest * stretch, stretch), stretch)
        term = dot_split(stacked, high, a_high[source, :, span], a_low[source, :, span], NN)
        z_own[dest] = z_own[dest] + term if k else term

    order = [far(k) * 2 + (1 - core) for k in range(1, n_y)] + [sibling]
    order += [far(k) * 2 + core for k in range(1, n_y)] + [row]
    mine = parts_of(col)
    for dest in order:
        back(0, dest, *mine)
    for k in range(1, n_col):
        other = lax.rem(col + k, n_col)
        for piece in range(pieces):
            arrived(hg.at[other, piece], h_recv.at[other, piece], {"col": other})
        theirs = parts_of(other)
        for place, dest in enumerate(order):
            back(k, dest, *theirs)
            if k == n_col - 1:
                ahead = place % n_y + 1
                spot = far(ahead)
                if place < n_y:
                    start(
                        z_own.at[dest], z_sib.at[spot], s_send.at[place], s_recv.at[spot],
                        {"row": sibling},
                    )
                elif place < n_row - 1:
                    arrived(z_sib.at[spot], s_recv.at[spot], {"row": sibling})
                    z_own[dest] = z_own[dest] + z_sib[spot]
                    start(
                        z_own.at[dest], z_far.at[y], f_send.at[ahead], f_recv.at[y], {"row": dest}
                    )

    w_sum = w_own[me]
    for k in range(1, peers):
        other, device = peer(k)
        arrived(w_in.at[other], w_recv.at[other], device)
        w_sum = w_sum + w_in[other]
    w_all[me] = w_sum * float(stretch * peers) ** (-0.5)
    for k in range(1, peers):
        other, device = peer(k)
        start(w_all.at[me], w_all.at[me], v_send.at[k], v_recv.at[me], device)

    arrived(z_sib.at[y], s_recv.at[y], {"row": sibling})
    total = z_own[row] + z_sib[y]
    for k in range(1, n_y):
        arrived(z_far.at[far(k)], f_recv.at[far(k)], {"row": far(k) * 2 + core})
        total = total + z_far[far(k)]
    input_grad[...] = total
    for k in range(1, peers):
        other, device = peer(k)
        arrived(w_all.at[other], v_recv.at[other], device)
    weight_grad[...] = w_all[...].reshape(weight_grad.shape)

    for copy in sent:
        copy.wait_send()
    for gap in range(n_rep - 1):
        for side in (1, -1):
            line_send(cg, c_send, c_recv, 0, gap, side, False)
            for piece in range(pieces):
                line_send(yg, y_send, y_recv, piece, gap, side, False)


def leave_kernel(*refs):
    count = (len(refs) - 1) // 2
    sems = refs[-1]
    copies = [
        pltpu.make_async_copy(refs[k], refs[count + k], sems.at[k]) for k in range(count)
    ]
    for copy in copies:
        copy.start()
    for copy in copies:
        copy.wait()


def leave(results):
    anywhere = pl.BlockSpec(memory_space=pl.ANY)
    return pl.pallas_call(
        leave_kernel,
        out_shape=tuple(jax.ShapeDtypeStruct(r.shape, r.dtype) for r in results),
        in_specs=[anywhere] * len(results),
        out_specs=(anywhere,) * len(results),
        scratch_shapes=[pltpu.SemaphoreType.DMA((len(results),))],
    )(*results)


def fused(
    n_row, n_col, n_rep, features, weight, cotangent, tile_values, tile_row, tile_col, tile_kind,
    tile_count,
):
    quarter, stretch = features.shape
    width = weight.shape[0]
    peers = n_row * n_col
    slots, edge, _ = tile_values.shape
    row_tiles, col_tiles = n_col * stretch // edge, n_row * stretch // edge
    parts = 8 if slots % 8 == 0 else 1
    dense = (n_col, stretch, n_row * stretch)
    pieces = 2 if stretch % (2 * edge) == 0 else 1
    cut = (pieces, quarter, stretch // pieces)
    block = (quarter, stretch)
    vmem = pl.BlockSpec(memory_space=pltpu.VMEM)
    smem = pl.BlockSpec(memory_space=pltpu.SMEM)
    dma = pltpu.SemaphoreType.DMA
    piece = (peers, quarter // peers, width)
    n_y = n_row // 2
    results = pl.pallas_call(
        functools.partial(layer_kernel, n_row, n_col, n_rep),
        out_shape=(
            jax.ShapeDtypeStruct(block, F32),
            jax.ShapeDtypeStruct(block, F32),
            jax.ShapeDtypeStruct((quarter, width), F32),
        ),
        in_specs=[smem] * 2 + [vmem] * 2 + [pl.BlockSpec(memory_space=pltpu.HBM)] * 4,
        out_specs=(vmem,) * 3,
        scratch_shapes=[
            pltpu.VMEM((1, slots), jnp.int32),
            pltpu.VMEM((1, row_tiles * col_tiles), jnp.int32),
            pltpu.SMEM((1, slots), jnp.int32),
            pltpu.SMEM((1, row_tiles * col_tiles), jnp.int32),
            pltpu.VMEM(tile_values.shape, F32),
            pltpu.VMEM((slots + 1, edge, edge), F32),
            pltpu.VMEM(weight.shape, F32),
            pltpu.VMEM(dense, BF16),
            pltpu.VMEM(dense, BF16),
            pltpu.VMEM((n_row * stretch, 2 * quarter), BF16),
            pltpu.VMEM((n_row, *block), F32),
            pltpu.VMEM((n_rep, 1, *block), F32),
            pltpu.VMEM((n_rep, *cut), F32),
            pltpu.VMEM((n_col, *cut), F32),
            pltpu.VMEM((n_col, *cut), F32),
            pltpu.VMEM((n_rep * quarter, stretch), F32),
            pltpu.VMEM((n_col, *cut), F32),
            pltpu.VMEM((n_row, *block), F32),
            pltpu.VMEM((n_y, *block), F32),
            pltpu.VMEM((n_y, *block), F32),
            pltpu.VMEM(piece, F32),
            pltpu.VMEM(piece, F32),
            pltpu.VMEM(piece, F32),
            dma((2,)), dma((3,)), dma((parts,)),
            dma((n_row,)), dma((n_row,)),
            dma((2, n_rep, 1)), dma((n_rep, 1)),
            dma((2, n_rep, pieces)), dma((n_rep, pieces)),
            dma((n_col, pieces)), dma((n_col, pieces)),
            dma((n_col, pieces)), dma((n_col, pieces)),
            dma((n_y,)), dma((n_y,)),
            dma((n_y,)), dma((n_y,)),
            dma((peers,)), dma((peers,)),
            dma((peers,)), dma((peers,)),
        ],
        compiler_params=pltpu.CompilerParams(
            collective_id=0, has_side_effects=True, vmem_limit_bytes=56 * 2**20
        ),
    )(tile_kind, tile_count, tile_row, tile_col, features, weight, cotangent, tile_values)
    return leave(results)


def tile_terms(source, values, from_tile, to_tile, tile_kinds, live_weight, dest_tiles, transposed):
    feat_width = source.shape[0]
    tile_edge = values.shape[1]
    tiled = source.reshape(feat_width, source.shape[1] // tile_edge, tile_edge)
    picked = jnp.take(tiled, from_tile, axis=1)
    chosen = jnp.take(values, tile_kinds, axis=0)
    if transposed:
        products = jnp.einsum("fga,gab->fgb", picked, chosen, precision=lax.Precision.HIGHEST)
    else:
        products = jnp.einsum("fgb,gab->fga", picked, chosen, precision=lax.Precision.HIGHEST)
    onehot = (to_tile[:, None] == jnp.arange(dest_tiles, dtype=jnp.int32)[None, :]).astype(
        jnp.float32
    )
    onehot = onehot * live_weight[:, None]
    spread = jnp.einsum("fgt,gd->fdt", products, onehot, precision=lax.Precision.HIGHEST)
    return spread.reshape(feat_width, dest_tiles * tile_edge)


def aggregate(source, values, from_tile, to_tile, tile_kinds, live_count, dest_tiles, transposed):
    slot_total = tile_kinds.shape[0]
    live_weight = (jnp.arange(slot_total, dtype=jnp.int32) < live_count).astype(jnp.float32)
    return tile_terms(
        source, values, from_tile, to_tile, tile_kinds, live_weight, dest_tiles, transposed
    )


def local(features, weight, cotangent, tile_values, tile_row, tile_col, tile_kind, tile_count):
    n_rowdev = lax.axis_size("row")
    n_coldev = lax.axis_size("col")
    n_repdev = lax.axis_size("rep")
    quarter, stretch_len = features.shape
    nodes = n_rowdev * n_coldev
    if (
        n_rowdev * n_coldev * stretch_len * stretch_len * 4 <= DENSE_BYTES
        and n_rowdev % 2 == 0
        and n_coldev > 1
        and n_repdev > 1
        and quarter % (8 * nodes) == 0
        and tile_values.size * 4 <= DENSE_BYTES
    ):
        return fused(
            n_rowdev, n_coldev, n_repdev, features, weight, cotangent, tile_values,
            tile_row, tile_col, tile_kind, tile_count,
        )
    own_rows = lax.dynamic_slice_in_dim(weight, lax.axis_index("rep") * quarter, quarter, 0)
    tile_edge = tile_values.shape[1]
    live_count = tile_count[0]
    row_tiles = n_coldev * stretch_len // tile_edge
    col_tiles = n_rowdev * stretch_len // tile_edge
    mixed = lax.psum_scatter(
        lax.dot_general(
            own_rows,
            features,
            (((0,), (0,)), ((), ())),
            precision=lax.Precision.HIGHEST,
            preferred_element_type=jnp.float32,
        ),
        "rep",
        scatter_dimension=0,
        tiled=True,
    )
    column_block = lax.all_gather(mixed, "row", axis=1, tiled=True)
    partial_value = aggregate(
        column_block, tile_values, tile_col, tile_row, tile_kind, live_count, row_tiles, False
    )
    summed = lax.psum_scatter(partial_value, "col", scatter_dimension=1, tiled=True)
    output, pullback = jax.vjp(lambda v: jax.nn.gelu(v, approximate=True), summed)
    (grad_pre,) = pullback(cotangent)
    row_block = lax.all_gather(grad_pre, "col", axis=1, tiled=True)
    partial_back = aggregate(
        row_block, tile_values, tile_row, tile_col, tile_kind, live_count, col_tiles, True
    )
    grad_mixed = lax.psum_scatter(partial_back, "row", scatter_dimension=1, tiled=True)
    whole = lax.all_gather(grad_mixed, "rep", axis=0, tiled=True)
    input_grad = jnp.dot(
        own_rows, whole, preferred_element_type=jnp.float32, precision=lax.Precision.HIGHEST
    )
    weight_part = lax.dot_general(
        features,
        whole,
        (((1,), (1,)), ((), ())),
        precision=lax.Precision.HIGHEST,
        preferred_element_type=jnp.float32,
    )
    node_total = stretch_len * n_rowdev * n_coldev
    weight_grad = lax.psum(weight_part * float(node_total) ** (-0.5), ("row", "col"))
    return (output, input_grad, weight_grad)


def solution(mesh):
    return jax.shard_map(
        local,
        mesh=mesh,
        in_specs=(
            P("rep", ("col", "row")),
            P(),
            P("rep", ("row", "col")),
            P(("row", "col"), None, None),
            P(("row", "col")),
            P(("row", "col")),
            P(("row", "col")),
            P(("row", "col")),
        ),
        out_specs=(P("rep", ("row", "col")), P("rep", ("col", "row")), P("rep", None)),
        check_vma=False,
    )
```

```python
import functools

import jax
import jax.numpy as jnp
from jax import lax
from jax.experimental import pallas as pl
from jax.experimental.pallas import tpu as pltpu
from jax.sharding import PartitionSpec as P

MESH = pl.DeviceIdType.MESH
F32, BF16 = jnp.float32, jnp.bfloat16
DENSE_BYTES = 16 * 2**20
NT = (((1,), (1,)), ((), ()))
NN = (((1,), (0,)), ((), ()))


def split(x):
    high = x.astype(BF16)
    return high, (x - high.astype(F32)).astype(BF16)


def dot_split(stacked, high, b_high, b_low, dims):
    rows = high.shape[0]
    both = lax.dot_general(stacked, b_high, dims, preferred_element_type=F32)
    cross = lax.dot_general(high, b_low, dims, preferred_element_type=F32)
    return both[:rows] + both[rows:] + cross


def product(a, b, dims):
    a_high, a_low = split(a)
    return dot_split(jnp.concatenate([a_high, a_low], 0), a_high, *split(b), dims)


def chain_links(row_tiles, col_tiles, count, tile_row, tile_col):
    slots = tile_row.shape[1]
    queries = slots + row_tiles * col_tiles
    place = tile_row * col_tiles + tile_col
    shape = (slots, slots)
    key, query = (lax.broadcasted_iota(jnp.int32, shape, axis) for axis in (0, 1))
    keys = jnp.max(jnp.where(key == query, place, 0), axis=1, keepdims=True)

    def latest(hit, key):
        last = jnp.max(jnp.where(hit & (key < count), key, -1), axis=0, keepdims=True)
        return jnp.where(last < 0, slots, last)

    before = latest((keys == place) & (key < query), key)
    shape = (slots, row_tiles * col_tiles)
    key, query = (lax.broadcasted_iota(jnp.int32, shape, axis) for axis in (0, 1))
    return before, latest(keys == query, key)


def layer_kernel(
    n_row, n_col, n_rep, kind, count, tile_row, tile_col, features_in, weight_in, cotangent_in, values_in,
    output, input_grad, weight_grad,
    before_v, last_v, before, last, held, chain, weight, a_high, a_low, xs, xg, cg, yg, part, part_in, pre, hg, z_own, z_sib, z_far, w_own, w_in, w_all,
    l_sem, i_sem, t_sem, x_send, x_recv, c_send, c_recv, y_send, y_recv, p_send, p_recv, h_send, h_recv,
    s_send, s_recv, f_send, f_recv, w_send, w_recv, v_send, v_recv,
):
    row, col, rep = lax.axis_index("row"), lax.axis_index("col"), lax.axis_index("rep")
    n_y = n_row // 2
    core, y = lax.rem(row, 2), lax.div(row, 2)
    sibling = y * 2 + (1 - core)
    quarter, stretch = features_in.shape
    slots, edge, _ = held.shape
    tiles = stretch // edge
    peers = n_row * n_col
    me = row * n_col + col

    def peer(k):
        other = lax.rem(me + k, peers)
        return other, {"row": lax.div(other, n_col), "col": lax.rem(other, n_col)}

    def far(k):
        return lax.rem(y + k, n_y)

    def send(src, dst, send_sem, recv_sem, device):
        return pltpu.make_async_remote_copy(
            src_ref=src, dst_ref=dst, send_sem=send_sem, recv_sem=recv_sem,
            device_id=device, device_id_type=MESH,
        )

    barrier = pltpu.get_barrier_semaphore()
    for k in range(1, peers):
        pl.semaphore_signal(barrier, inc=1, device_id=peer(k)[1], device_id_type=MESH)

    @pl.when(rep > 0)
    def _():
        pl.semaphore_signal(barrier, inc=1, device_id={"rep": rep - 1}, device_id_type=MESH)

    @pl.when(rep < n_rep - 1)
    def _():
        pl.semaphore_signal(barrier, inc=1, device_id={"rep": rep + 1}, device_id_type=MESH)

    inputs = [
        pltpu.make_async_copy(features_in, xg.at[row], i_sem.at[0]),
        pltpu.make_async_copy(cotangent_in, cg.at[rep, 0], i_sem.at[1]),
        pltpu.make_async_copy(weight_in, weight, i_sem.at[2]),
    ]
    parts = t_sem.shape[0]
    size = slots // parts
    for k in range(parts):
        piece = pl.ds(k * size, size)
        inputs.append(pltpu.make_async_copy(values_in.at[piece], held.at[piece], t_sem.at[k]))
    for copy in inputs:
        copy.start()

    ends = jnp.where(rep == 0, 1, 0) + jnp.where(rep == n_rep - 1, 1, 0)
    pl.semaphore_wait(barrier, peers + 1 - ends)

    sent = []

    def start(*args):
        copy = send(*args)
        copy.start()
        sent.append(copy)

    def line_send(buf, send_sem, recv_sem, piece, gap, side, begin):
        origin = rep - gap * side
        go = (origin >= 0) & (origin < n_rep) & (rep + side >= 0) & (rep + side < n_rep)

        @pl.when(go)
        def _():
            copy = send(
                buf.at[origin, piece], buf.at[origin, piece],
                send_sem.at[(side + 1) // 2, gap, piece], recv_sem.at[origin, piece],
                {"rep": rep + side},
            )
            if begin:
                copy.start()
            else:
                copy.wait_send()

    def line_step(buf, send_sem, recv_sem, piece, gap):
        for side in (1, -1):
            if gap:
                origin = rep - gap * side

                @pl.when((origin >= 0) & (origin < n_rep))
                def _():
                    send(
                        buf.at[origin, piece], buf.at[origin, piece], send_sem.at[0, 0, 0],
                        recv_sem.at[origin, piece], {"rep": rep - side},
                    ).wait_recv()

            if gap < n_rep - 1:
                line_send(buf, send_sem, recv_sem, piece, gap, side, True)

    def arrived(buf, recv_sem, device):
        send(buf, buf, x_send.at[0], recv_sem, device).wait_recv()

    inputs[0].wait()
    for k in range(1, n_y):
        start(xg.at[row], xg.at[row], x_send.at[k], x_recv.at[row], {"row": far(k) * 2 + core})
    start(xg.at[row], xg.at[row], x_send.at[0], x_recv.at[row], {"row": sibling})
    inputs[1].wait()
    line_step(cg, c_send, c_recv, 0, 0)

    links = chain_links(
        n_col * tiles, n_row * tiles, count[0],
        tile_row[...].reshape(1, slots), tile_col[...].reshape(1, slots),
    )
    before_v[...], last_v[...] = links
    moves = [
        pltpu.make_async_copy(before_v, before, l_sem.at[0]),
        pltpu.make_async_copy(last_v, last, l_sem.at[1]),
    ]
    for copy in moves:
        copy.start()

    for copy in inputs[2:] + moves:
        copy.wait()
    chain[slots] = jnp.zeros((edge, edge), F32)

    @pl.loop(0, slots, unroll=4 if slots % 4 == 0 else 1)
    def _(slot):
        chain[slot] = held[kind[slot]] + chain[before[0, slot]]

    def ready(origin):
        high, low = split(xg[origin])
        both = jnp.concatenate([high.astype(F32), low.astype(F32)], 0).T
        xs[pl.ds(pl.multiple_of(origin * stretch, stretch), stretch), :] = both.astype(BF16)

    ready(row)
    for k in range(1, n_y):
        origin = far(k) * 2 + core
        arrived(xg.at[origin], x_recv.at[origin], {"row": origin})
        start(
            xg.at[origin], xg.at[origin], x_send.at[n_y + k - 1], x_recv.at[origin],
            {"row": sibling},
        )
        ready(origin)
    arrived(xg.at[sibling], x_recv.at[sibling], {"row": sibling})
    ready(sibling)
    line_step(cg, c_send, c_recv, 0, 1)

    pieces = yg.shape[1]
    short = stretch // pieces
    spans = [pl.ds(piece * short, short) for piece in range(pieces)]

    def dense(dest, piece):
        @pl.loop(0, short // edge)
        def _(i):
            first = (dest * tiles + piece * (short // edge) + i) * (n_row * tiles)
            rows = pl.ds(pl.multiple_of(piece * short + i * edge, edge), edge)
            for j in range(n_row * tiles):
                high, low = split(chain[last[0, first + j]])
                a_high[dest, rows, pl.ds(j * edge, edge)] = high
                a_low[dest, rows, pl.ds(j * edge, edge)] = low

    def aggregate_piece(dest, piece):
        nodes = xs[...]
        term = jnp.dot(a_high[dest, spans[piece], :], nodes, preferred_element_type=F32)
        term += jnp.dot(a_low[dest, spans[piece], :], nodes, preferred_element_type=F32)
        term = term.T
        return term[:quarter] + term[quarter:]

    def others(piece):
        for k in range(1, n_col):
            dest = lax.rem(col + k, n_col)
            dense(dest, piece)
            if k == 1 and piece == 0:
                for far_y in range(1, n_y):
                    origin = far(far_y) * 2 + (1 - core)
                    arrived(xg.at[origin], x_recv.at[origin], {"row": sibling})
                    ready(origin)
            part[dest, piece] = aggregate_piece(dest, piece)
            start(
                part.at[dest, piece], part_in.at[col, piece], p_send.at[k, piece],
                p_recv.at[col, piece], {"col": dest},
            )

    def own_part(piece):
        dense(col, piece)
        summed = aggregate_piece(col, piece)
        for k in range(1, n_col):
            other = lax.rem(col + k, n_col)
            arrived(part_in.at[other, piece], p_recv.at[other, piece], {"col": other})
            summed = summed + part_in[other, piece]
        yg[rep, piece] = summed
        line_step(yg, y_send, y_recv, piece, 0)

    others(0)
    for gap in range(2, n_rep - 1):
        line_step(cg, c_send, c_recv, 0, gap)
    for piece in range(pieces):
        if piece + 1 < pieces:
            others(piece + 1)
        own_part(piece)
        if piece >= 2:
            line_step(yg, y_send, y_recv, piece - 2, 1)
    if n_rep > 2:
        line_step(cg, c_send, c_recv, 0, n_rep - 1)
    turned = weight[...].T
    t_high, t_low = split(turned)
    t_both = jnp.concatenate([t_high, t_low], 0)
    own = weight[pl.ds(pl.multiple_of(rep * quarter, quarter), quarter), :]
    o_high, o_low = split(own)
    o_both = jnp.concatenate([o_high, o_low], 0)
    scale = (2.0 / 3.141592653589793) ** 0.5

    def bend(v):
        return jnp.tanh(scale * (v + 0.044715 * (v * v * v)))

    w_part = None
    width = n_rep * quarter
    steps = [(piece + 2 * gap, gap, piece) for gap in range(1, n_rep) for piece in range(pieces)]
    for _, gap, piece in sorted(steps):
        if gap > 1 or piece + 2 >= pieces:
            line_step(yg, y_send, y_recv, piece, gap)
        if gap < n_rep - 1:
            continue
        gathered = jnp.concatenate([yg[origin, piece] for origin in range(n_rep)], 0)
        v = dot_split(t_both, t_high, *split(gathered), NN)
        pre[:, spans[piece]] = v
        t = bend(v)
        slope = 0.5 * (1.0 + t) + 0.5 * v * (1.0 - t * t) * (scale * (1.0 + 0.134145 * (v * v)))
        grad_pre = cg[:, 0, :, spans[piece]].reshape(width, short) * slope
        g_high, g_low = split(grad_pre)
        hg[col, piece] = dot_split(o_both, o_high, g_high, g_low, NN)
        for k in range(1, n_col):
            other = lax.rem(col + k, n_col)
            start(
                hg.at[col, piece], hg.at[col, piece], h_send.at[k, piece], h_recv.at[col, piece],
                {"col": other},
            )
        y_high, y_low = split(yg[rep, piece])
        term = dot_split(jnp.concatenate([y_high, y_low], 0), y_high, g_high, g_low, NT)
        w_part = term if w_part is None else w_part + term

    w_own[...] = w_part.reshape(w_own.shape)
    for k in range(1, peers):
        other, device = peer(k)
        start(w_own.at[other], w_in.at[me], w_send.at[k], w_recv.at[me], device)
    mine = pre[pl.ds(pl.multiple_of(rep * quarter, quarter), quarter), :]
    output[...] = 0.5 * mine * (1.0 + bend(mine))

    def parts_of(source):
        high, low = split(jnp.concatenate([hg[source, piece] for piece in range(pieces)], 1))
        return jnp.concatenate([high, low], 0), high

    def back(k, dest, stacked, high):
        source = lax.rem(col + k, n_col)
        span = pl.ds(pl.multiple_of(dest * stretch, stretch), stretch)
        term = dot_split(stacked, high, a_high[source, :, span], a_low[source, :, span], NN)
        z_own[dest] = z_own[dest] + term if k else term

    order = [far(k) * 2 + (1 - core) for k in range(1, n_y)] + [sibling]
    order += [far(k) * 2 + core for k in range(1, n_y)] + [row]
    mine = parts_of(col)
    for dest in order:
        back(0, dest, *mine)
    for k in range(1, n_col):
        other = lax.rem(col + k, n_col)
        for piece in range(pieces):
            arrived(hg.at[other, piece], h_recv.at[other, piece], {"col": other})
        theirs = parts_of(other)
        for place, dest in enumerate(order):
            back(k, dest, *theirs)
            if k == n_col - 1:
                ahead = place % n_y + 1
                spot = far(ahead)
                if place < n_y:
                    start(
                        z_own.at[dest], z_sib.at[spot], s_send.at[place], s_recv.at[spot],
                        {"row": sibling},
                    )
                elif place < n_row - 1:
                    arrived(z_sib.at[spot], s_recv.at[spot], {"row": sibling})
                    z_own[dest] = z_own[dest] + z_sib[spot]
                    start(
                        z_own.at[dest], z_far.at[y], f_send.at[ahead], f_recv.at[y], {"row": dest}
                    )

    w_sum = w_own[me]
    for k in range(1, peers):
        other, device = peer(k)
        arrived(w_in.at[other], w_recv.at[other], device)
        w_sum = w_sum + w_in[other]
    w_all[me] = w_sum * float(stretch * peers) ** (-0.5)
    for k in range(1, peers):
        other, device = peer(k)
        start(w_all.at[me], w_all.at[me], v_send.at[k], v_recv.at[me], device)

    arrived(z_sib.at[y], s_recv.at[y], {"row": sibling})
    total = z_own[row] + z_sib[y]
    for k in range(1, n_y):
        arrived(z_far.at[far(k)], f_recv.at[far(k)], {"row": far(k) * 2 + core})
        total = total + z_far[far(k)]
    input_grad[...] = total
    for k in range(1, peers):
        other, device = peer(k)
        arrived(w_all.at[other], v_recv.at[other], device)
    weight_grad[...] = w_all[...].reshape(weight_grad.shape)

    for copy in sent:
        copy.wait_send()
    for gap in range(n_rep - 1):
        for side in (1, -1):
            line_send(cg, c_send, c_recv, 0, gap, side, False)
            for piece in range(pieces):
                line_send(yg, y_send, y_recv, piece, gap, side, False)


def leave_kernel(*refs):
    count = len(refs) // 2
    for k in range(count):
        refs[count + k][...] = refs[k][...]


def leave(results):
    vmem = pl.BlockSpec(memory_space=pltpu.VMEM)
    return pl.pallas_call(
        leave_kernel,
        out_shape=tuple(jax.ShapeDtypeStruct(r.shape, r.dtype) for r in results),
        in_specs=[vmem] * len(results),
        out_specs=(vmem,) * len(results),
    )(*results)


def fused(
    n_row, n_col, n_rep, features, weight, cotangent, tile_values, tile_row, tile_col, tile_kind,
    tile_count,
):
    quarter, stretch = features.shape
    width = weight.shape[0]
    peers = n_row * n_col
    slots, edge, _ = tile_values.shape
    row_tiles, col_tiles = n_col * stretch // edge, n_row * stretch // edge
    parts = 8 if slots % 8 == 0 else 1
    dense = (n_col, stretch, n_row * stretch)
    pieces = stretch // edge
    cut = (pieces, quarter, stretch // pieces)
    block = (quarter, stretch)
    vmem = pl.BlockSpec(memory_space=pltpu.VMEM)
    smem = pl.BlockSpec(memory_space=pltpu.SMEM)
    dma = pltpu.SemaphoreType.DMA
    piece = (peers, quarter // peers, width)
    n_y = n_row // 2
    results = pl.pallas_call(
        functools.partial(layer_kernel, n_row, n_col, n_rep),
        out_shape=(
            jax.ShapeDtypeStruct(block, F32),
            jax.ShapeDtypeStruct(block, F32),
            jax.ShapeDtypeStruct((quarter, width), F32),
        ),
        in_specs=[smem] * 2 + [vmem] * 2 + [pl.BlockSpec(memory_space=pltpu.HBM)] * 4,
        out_specs=(vmem,) * 3,
        scratch_shapes=[
            pltpu.VMEM((1, slots), jnp.int32),
            pltpu.VMEM((1, row_tiles * col_tiles), jnp.int32),
            pltpu.SMEM((1, slots), jnp.int32),
            pltpu.SMEM((1, row_tiles * col_tiles), jnp.int32),
            pltpu.VMEM(tile_values.shape, F32),
            pltpu.VMEM((slots + 1, edge, edge), F32),
            pltpu.VMEM(weight.shape, F32),
            pltpu.VMEM(dense, BF16),
            pltpu.VMEM(dense, BF16),
            pltpu.VMEM((n_row * stretch, 2 * quarter), BF16),
            pltpu.VMEM((n_row, *block), F32),
            pltpu.VMEM((n_rep, 1, *block), F32),
            pltpu.VMEM((n_rep, *cut), F32),
            pltpu.VMEM((n_col, *cut), F32),
            pltpu.VMEM((n_col, *cut), F32),
            pltpu.VMEM((n_rep * quarter, stretch), F32),
            pltpu.VMEM((n_col, *cut), F32),
            pltpu.VMEM((n_row, *block), F32),
            pltpu.VMEM((n_y, *block), F32),
            pltpu.VMEM((n_y, *block), F32),
            pltpu.VMEM(piece, F32),
            pltpu.VMEM(piece, F32),
            pltpu.VMEM(piece, F32),
            dma((2,)), dma((3,)), dma((parts,)),
            dma((n_row,)), dma((n_row,)),
            dma((2, n_rep, 1)), dma((n_rep, 1)),
            dma((2, n_rep, pieces)), dma((n_rep, pieces)),
            dma((n_col, pieces)), dma((n_col, pieces)),
            dma((n_col, pieces)), dma((n_col, pieces)),
            dma((n_y,)), dma((n_y,)),
            dma((n_y,)), dma((n_y,)),
            dma((peers,)), dma((peers,)),
            dma((peers,)), dma((peers,)),
        ],
        compiler_params=pltpu.CompilerParams(
            collective_id=0, has_side_effects=True, vmem_limit_bytes=56 * 2**20
        ),
    )(tile_kind, tile_count, tile_row, tile_col, features, weight, cotangent, tile_values)
    return leave(results)


def tile_terms(source, values, from_tile, to_tile, tile_kinds, live_weight, dest_tiles, transposed):
    feat_width = source.shape[0]
    tile_edge = values.shape[1]
    tiled = source.reshape(feat_width, source.shape[1] // tile_edge, tile_edge)
    picked = jnp.take(tiled, from_tile, axis=1)
    chosen = jnp.take(values, tile_kinds, axis=0)
    if transposed:
        products = jnp.einsum("fga,gab->fgb", picked, chosen, precision=lax.Precision.HIGHEST)
    else:
        products = jnp.einsum("fgb,gab->fga", picked, chosen, precision=lax.Precision.HIGHEST)
    onehot = (to_tile[:, None] == jnp.arange(dest_tiles, dtype=jnp.int32)[None, :]).astype(
        jnp.float32
    )
    onehot = onehot * live_weight[:, None]
    spread = jnp.einsum("fgt,gd->fdt", products, onehot, precision=lax.Precision.HIGHEST)
    return spread.reshape(feat_width, dest_tiles * tile_edge)


def aggregate(source, values, from_tile, to_tile, tile_kinds, live_count, dest_tiles, transposed):
    slot_total = tile_kinds.shape[0]
    live_weight = (jnp.arange(slot_total, dtype=jnp.int32) < live_count).astype(jnp.float32)
    return tile_terms(
        source, values, from_tile, to_tile, tile_kinds, live_weight, dest_tiles, transposed
    )


def local(features, weight, cotangent, tile_values, tile_row, tile_col, tile_kind, tile_count):
    n_rowdev = lax.axis_size("row")
    n_coldev = lax.axis_size("col")
    n_repdev = lax.axis_size("rep")
    quarter, stretch_len = features.shape
    nodes = n_rowdev * n_coldev
    if (
        n_rowdev * n_coldev * stretch_len * stretch_len * 4 <= DENSE_BYTES
        and n_rowdev % 2 == 0
        and n_coldev > 1
        and n_repdev > 1
        and quarter % (8 * nodes) == 0
        and tile_values.size * 4 <= DENSE_BYTES
    ):
        return fused(
            n_rowdev, n_coldev, n_repdev, features, weight, cotangent, tile_values,
            tile_row, tile_col, tile_kind, tile_count,
        )
    own_rows = lax.dynamic_slice_in_dim(weight, lax.axis_index("rep") * quarter, quarter, 0)
    tile_edge = tile_values.shape[1]
    live_count = tile_count[0]
    row_tiles = n_coldev * stretch_len // tile_edge
    col_tiles = n_rowdev * stretch_len // tile_edge
    mixed = lax.psum_scatter(
        lax.dot_general(
            own_rows,
            features,
            (((0,), (0,)), ((), ())),
            precision=lax.Precision.HIGHEST,
            preferred_element_type=jnp.float32,
        ),
        "rep",
        scatter_dimension=0,
        tiled=True,
    )
    column_block = lax.all_gather(mixed, "row", axis=1, tiled=True)
    partial_value = aggregate(
        column_block, tile_values, tile_col, tile_row, tile_kind, live_count, row_tiles, False
    )
    summed = lax.psum_scatter(partial_value, "col", scatter_dimension=1, tiled=True)
    output, pullback = jax.vjp(lambda v: jax.nn.gelu(v, approximate=True), summed)
    (grad_pre,) = pullback(cotangent)
    row_block = lax.all_gather(grad_pre, "col", axis=1, tiled=True)
    partial_back = aggregate(
        row_block, tile_values, tile_row, tile_col, tile_kind, live_count, col_tiles, True
    )
    grad_mixed = lax.psum_scatter(partial_back, "row", scatter_dimension=1, tiled=True)
    whole = lax.all_gather(grad_mixed, "rep", axis=0, tiled=True)
    input_grad = jnp.dot(
        own_rows, whole, preferred_element_type=jnp.float32, precision=lax.Precision.HIGHEST
    )
    weight_part = lax.dot_general(
        features,
        whole,
        (((1,), (1,)), ((), ())),
        precision=lax.Precision.HIGHEST,
        preferred_element_type=jnp.float32,
    )
    node_total = stretch_len * n_rowdev * n_coldev
    weight_grad = lax.psum(weight_part * float(node_total) ** (-0.5), ("row", "col"))
    return (output, input_grad, weight_grad)


def solution(mesh):
    return jax.shard_map(
        local,
        mesh=mesh,
        in_specs=(
            P("rep", ("col", "row")),
            P(),
            P("rep", ("row", "col")),
            P(("row", "col"), None, None),
            P(("row", "col")),
            P(("row", "col")),
            P(("row", "col")),
            P(("row", "col")),
        ),
        out_specs=(P("rep", ("row", "col")), P("rep", ("col", "row")), P("rep", None)),
        check_vma=False,
    )
```

```python
import functools

import jax
import jax.numpy as jnp
from jax import lax
from jax.experimental import pallas as pl
from jax.experimental.pallas import tpu as pltpu
from jax.sharding import PartitionSpec as P

MESH = pl.DeviceIdType.MESH
F32, BF16 = jnp.float32, jnp.bfloat16
DENSE_BYTES = 16 * 2**20
NT = (((1,), (1,)), ((), ()))
NN = (((1,), (0,)), ((), ()))


def split(x):
    high = x.astype(BF16)
    return high, (x - high.astype(F32)).astype(BF16)


def dot_split(stacked, high, b_high, b_low, dims):
    rows = high.shape[0]
    both = lax.dot_general(stacked, b_high, dims, preferred_element_type=F32)
    cross = lax.dot_general(high, b_low, dims, preferred_element_type=F32)
    return both[:rows] + both[rows:] + cross


def product(a, b, dims):
    a_high, a_low = split(a)
    return dot_split(jnp.concatenate([a_high, a_low], 0), a_high, *split(b), dims)


def chain_links(row_tiles, col_tiles, count, tile_row, tile_col):
    slots = tile_row.shape[1]
    queries = slots + row_tiles * col_tiles
    place = tile_row * col_tiles + tile_col
    shape = (slots, slots)
    key, query = (lax.broadcasted_iota(jnp.int32, shape, axis) for axis in (0, 1))
    keys = jnp.max(jnp.where(key == query, place, 0), axis=1, keepdims=True)

    def latest(hit, key):
        last = jnp.max(jnp.where(hit & (key < count), key, -1), axis=0, keepdims=True)
        return jnp.where(last < 0, slots, last)

    before = latest((keys == place) & (key < query), key)
    shape = (slots, row_tiles * col_tiles)
    key, query = (lax.broadcasted_iota(jnp.int32, shape, axis) for axis in (0, 1))
    return before, latest(keys == query, key)


def layer_kernel(
    n_row, n_col, n_rep, kind, count, tile_row, tile_col, features_in, weight_in, cotangent_in, values_in,
    output, input_grad, weight_grad,
    before_v, last_v, before, last, held, chain, weight, a_high, a_low, xs, xg, cg, yg, part, part_in, pre, hg, z_own, z_sib, z_far, w_own, w_in, w_all,
    l_sem, i_sem, t_sem, x_send, x_recv, c_send, c_recv, y_send, y_recv, p_send, p_recv, h_send, h_recv,
    s_send, s_recv, f_send, f_recv, w_send, w_recv, v_send, v_recv,
):
    row, col, rep = lax.axis_index("row"), lax.axis_index("col"), lax.axis_index("rep")
    n_y = n_row // 2
    core, y = lax.rem(row, 2), lax.div(row, 2)
    sibling = y * 2 + (1 - core)
    quarter, stretch = features_in.shape
    slots, edge, _ = held.shape
    tiles = stretch // edge
    peers = n_row * n_col
    me = row * n_col + col

    def peer(k):
        other = lax.rem(me + k, peers)
        return other, {"row": lax.div(other, n_col), "col": lax.rem(other, n_col)}

    def far(k):
        return lax.rem(y + k, n_y)

    def send(src, dst, send_sem, recv_sem, device):
        return pltpu.make_async_remote_copy(
            src_ref=src, dst_ref=dst, send_sem=send_sem, recv_sem=recv_sem,
            device_id=device, device_id_type=MESH,
        )

    barrier = pltpu.get_barrier_semaphore()
    for k in range(1, peers):
        pl.semaphore_signal(barrier, inc=1, device_id=peer(k)[1], device_id_type=MESH)

    @pl.when(rep > 0)
    def _():
        pl.semaphore_signal(barrier, inc=1, device_id={"rep": rep - 1}, device_id_type=MESH)

    @pl.when(rep < n_rep - 1)
    def _():
        pl.semaphore_signal(barrier, inc=1, device_id={"rep": rep + 1}, device_id_type=MESH)

    inputs = [
        pltpu.make_async_copy(features_in, xg.at[row], i_sem.at[0]),
        pltpu.make_async_copy(cotangent_in, cg.at[rep, 0], i_sem.at[1]),
        pltpu.make_async_copy(weight_in, weight, i_sem.at[2]),
    ]
    parts = t_sem.shape[0]
    size = slots // parts
    for k in range(parts):
        piece = pl.ds(k * size, size)
        inputs.append(pltpu.make_async_copy(values_in.at[piece], held.at[piece], t_sem.at[k]))
    for copy in inputs:
        copy.start()

    ends = jnp.where(rep == 0, 1, 0) + jnp.where(rep == n_rep - 1, 1, 0)
    pl.semaphore_wait(barrier, peers + 1 - ends)

    sent = []

    def start(*args):
        copy = send(*args)
        copy.start()
        sent.append(copy)

    def line_send(buf, send_sem, recv_sem, piece, gap, side, begin):
        origin = rep - gap * side
        go = (origin >= 0) & (origin < n_rep) & (rep + side >= 0) & (rep + side < n_rep)

        @pl.when(go)
        def _():
            copy = send(
                buf.at[origin, piece], buf.at[origin, piece],
                send_sem.at[(side + 1) // 2, gap, piece], recv_sem.at[origin, piece],
                {"rep": rep + side},
            )
            if begin:
                copy.start()
            else:
                copy.wait_send()

    def line_step(buf, send_sem, recv_sem, piece, gap):
        for side in (1, -1):
            if gap:
                origin = rep - gap * side

                @pl.when((origin >= 0) & (origin < n_rep))
                def _():
                    send(
                        buf.at[origin, piece], buf.at[origin, piece], send_sem.at[0, 0, 0],
                        recv_sem.at[origin, piece], {"rep": rep - side},
                    ).wait_recv()

            if gap < n_rep - 1:
                line_send(buf, send_sem, recv_sem, piece, gap, side, True)

    def arrived(buf, recv_sem, device):
        send(buf, buf, x_send.at[0], recv_sem, device).wait_recv()

    inputs[0].wait()
    for k in range(1, n_y):
        start(xg.at[row], xg.at[row], x_send.at[k], x_recv.at[row], {"row": far(k) * 2 + core})
    start(xg.at[row], xg.at[row], x_send.at[0], x_recv.at[row], {"row": sibling})
    inputs[1].wait()
    line_step(cg, c_send, c_recv, 0, 0)

    links = chain_links(
        n_col * tiles, n_row * tiles, count[0],
        tile_row[...].reshape(1, slots), tile_col[...].reshape(1, slots),
    )
    before_v[...], last_v[...] = links
    moves = [
        pltpu.make_async_copy(before_v, before, l_sem.at[0]),
        pltpu.make_async_copy(last_v, last, l_sem.at[1]),
    ]
    for copy in moves:
        copy.start()

    for copy in inputs[2:] + moves:
        copy.wait()
    chain[slots] = jnp.zeros((edge, edge), F32)

    @pl.loop(0, slots, unroll=8 if slots % 8 == 0 else 1)
    def _(slot):
        chain[slot] = held[kind[slot]] + chain[before[0, slot]]

    def ready(origin):
        high, low = split(xg[origin])
        both = jnp.concatenate([high.astype(F32), low.astype(F32)], 0).T
        xs[pl.ds(pl.multiple_of(origin * stretch, stretch), stretch), :] = both.astype(BF16)

    ready(row)
    for k in range(1, n_y):
        origin = far(k) * 2 + core
        arrived(xg.at[origin], x_recv.at[origin], {"row": origin})
        start(
            xg.at[origin], xg.at[origin], x_send.at[n_y + k - 1], x_recv.at[origin],
            {"row": sibling},
        )
        ready(origin)
    arrived(xg.at[sibling], x_recv.at[sibling], {"row": sibling})
    ready(sibling)
    line_step(cg, c_send, c_recv, 0, 1)

    pieces = yg.shape[1]
    short = stretch // pieces
    spans = [pl.ds(piece * short, short) for piece in range(pieces)]

    def dense(dest, piece):
        @pl.loop(0, short // edge)
        def _(i):
            first = (dest * tiles + piece * (short // edge) + i) * (n_row * tiles)
            rows = pl.ds(pl.multiple_of(piece * short + i * edge, edge), edge)
            for j in range(n_row * tiles):
                high, low = split(chain[last[0, first + j]])
                a_high[dest, rows, pl.ds(j * edge, edge)] = high
                a_low[dest, rows, pl.ds(j * edge, edge)] = low

    def aggregate_piece(dest, piece):
        nodes = xs[...]
        rows = jnp.concatenate(
            [a_high[dest, spans[piece], :], a_low[dest, spans[piece], :]], 0
        )
        term = jnp.dot(rows, nodes, preferred_element_type=F32)
        term = term[:short] + term[short:]
        term = term.T
        return term[:quarter] + term[quarter:]

    def others(piece):
        for k in range(1, n_col):
            dest = lax.rem(col + k, n_col)
            dense(dest, piece)
            if k == 1 and piece == 0:
                for far_y in range(1, n_y):
                    origin = far(far_y) * 2 + (1 - core)
                    arrived(xg.at[origin], x_recv.at[origin], {"row": sibling})
                    ready(origin)
            part[dest, piece] = aggregate_piece(dest, piece)
            start(
                part.at[dest, piece], part_in.at[col, piece], p_send.at[k, piece],
                p_recv.at[col, piece], {"col": dest},
            )

    def own_part(piece):
        dense(col, piece)
        summed = aggregate_piece(col, piece)
        for k in range(1, n_col):
            other = lax.rem(col + k, n_col)
            arrived(part_in.at[other, piece], p_recv.at[other, piece], {"col": other})
            summed = summed + part_in[other, piece]
        yg[rep, piece] = summed
        line_step(yg, y_send, y_recv, piece, 0)

    others(0)
    for gap in range(2, n_rep - 1):
        line_step(cg, c_send, c_recv, 0, gap)
    for piece in range(pieces):
        if piece + 1 < pieces:
            others(piece + 1)
        own_part(piece)
        if piece >= 2:
            line_step(yg, y_send, y_recv, piece - 2, 1)
    if n_rep > 2:
        line_step(cg, c_send, c_recv, 0, n_rep - 1)
    turned = weight[...].T
    t_high, t_low = split(turned)
    t_both = jnp.concatenate([t_high, t_low], 0)
    own = weight[pl.ds(pl.multiple_of(rep * quarter, quarter), quarter), :]
    o_high, o_low = split(own)
    o_both = jnp.concatenate([o_high, o_low], 0)
    scale = (2.0 / 3.141592653589793) ** 0.5

    def bend(v):
        return jnp.tanh(scale * (v + 0.044715 * (v * v * v)))

    w_part = None
    width = n_rep * quarter
    steps = [(piece + 2 * gap, gap, piece) for gap in range(1, n_rep) for piece in range(pieces)]
    for _, gap, piece in sorted(steps):
        if gap > 1 or piece + 2 >= pieces:
            line_step(yg, y_send, y_recv, piece, gap)
        if gap < n_rep - 1:
            continue
        gathered = jnp.concatenate([yg[origin, piece] for origin in range(n_rep)], 0)
        v = dot_split(t_both, t_high, *split(gathered), NN)
        pre[:, spans[piece]] = v
        t = bend(v)
        slope = 0.5 * (1.0 + t) + 0.5 * v * (1.0 - t * t) * (scale * (1.0 + 0.134145 * (v * v)))
        grad_pre = cg[:, 0, :, spans[piece]].reshape(width, short) * slope
        g_high, g_low = split(grad_pre)
        hg[col, piece] = dot_split(o_both, o_high, g_high, g_low, NN)
        for k in range(1, n_col):
            other = lax.rem(col + k, n_col)
            start(
                hg.at[col, piece], hg.at[col, piece], h_send.at[k, piece], h_recv.at[col, piece],
                {"col": other},
            )
        y_high, y_low = split(yg[rep, piece])
        term = dot_split(jnp.concatenate([y_high, y_low], 0), y_high, g_high, g_low, NT)
        w_part = term if w_part is None else w_part + term

    w_own[...] = w_part.reshape(w_own.shape)
    for k in range(1, peers):
        other, device = peer(k)
        start(w_own.at[other], w_in.at[me], w_send.at[k], w_recv.at[me], device)
    mine = pre[pl.ds(pl.multiple_of(rep * quarter, quarter), quarter), :]
    output[...] = 0.5 * mine * (1.0 + bend(mine))

    def parts_of(source):
        high, low = split(jnp.concatenate([hg[source, piece] for piece in range(pieces)], 1))
        return jnp.concatenate([high, low], 0), high

    def back(k, dest, stacked, high):
        source = lax.rem(col + k, n_col)
        span = pl.ds(pl.multiple_of(dest * stretch, stretch), stretch)
        term = dot_split(stacked, high, a_high[source, :, span], a_low[source, :, span], NN)
        z_own[dest] = z_own[dest] + term if k else term

    order = [far(k) * 2 + (1 - core) for k in range(1, n_y)] + [sibling]
    order += [far(k) * 2 + core for k in range(1, n_y)] + [row]
    mine = parts_of(col)
    for dest in order:
        back(0, dest, *mine)
    for k in range(1, n_col):
        other = lax.rem(col + k, n_col)
        for piece in range(pieces):
            arrived(hg.at[other, piece], h_recv.at[other, piece], {"col": other})
        theirs = parts_of(other)
        for place, dest in enumerate(order):
            back(k, dest, *theirs)
            if k == n_col - 1:
                ahead = place % n_y + 1
                spot = far(ahead)
                if place < n_y:
                    start(
                        z_own.at[dest], z_sib.at[spot], s_send.at[place], s_recv.at[spot],
                        {"row": sibling},
                    )
                elif place < n_row - 1:
                    arrived(z_sib.at[spot], s_recv.at[spot], {"row": sibling})
                    z_own[dest] = z_own[dest] + z_sib[spot]
                    start(
                        z_own.at[dest], z_far.at[y], f_send.at[ahead], f_recv.at[y], {"row": dest}
                    )

    w_sum = w_own[me]
    for k in range(1, peers):
        other, device = peer(k)
        arrived(w_in.at[other], w_recv.at[other], device)
        w_sum = w_sum + w_in[other]
    w_all[me] = w_sum * float(stretch * peers) ** (-0.5)
    for k in range(1, peers):
        other, device = peer(k)
        start(w_all.at[me], w_all.at[me], v_send.at[k], v_recv.at[me], device)

    arrived(z_sib.at[y], s_recv.at[y], {"row": sibling})
    total = z_own[row] + z_sib[y]
    for k in range(1, n_y):
        arrived(z_far.at[far(k)], f_recv.at[far(k)], {"row": far(k) * 2 + core})
        total = total + z_far[far(k)]
    input_grad[...] = total
    for k in range(1, peers):
        other, device = peer(k)
        arrived(w_all.at[other], v_recv.at[other], device)
    weight_grad[...] = w_all[...].reshape(weight_grad.shape)

    for copy in sent:
        copy.wait_send()
    for gap in range(n_rep - 1):
        for side in (1, -1):
            line_send(cg, c_send, c_recv, 0, gap, side, False)
            for piece in range(pieces):
                line_send(yg, y_send, y_recv, piece, gap, side, False)


def leave_kernel(*refs):
    count = len(refs) // 2
    for k in range(count):
        refs[count + k][...] = refs[k][...]


def leave(results):
    vmem = pl.BlockSpec(memory_space=pltpu.VMEM)
    return pl.pallas_call(
        leave_kernel,
        out_shape=tuple(jax.ShapeDtypeStruct(r.shape, r.dtype) for r in results),
        in_specs=[vmem] * len(results),
        out_specs=(vmem,) * len(results),
    )(*results)


def fused(
    n_row, n_col, n_rep, features, weight, cotangent, tile_values, tile_row, tile_col, tile_kind,
    tile_count,
):
    quarter, stretch = features.shape
    width = weight.shape[0]
    peers = n_row * n_col
    slots, edge, _ = tile_values.shape
    row_tiles, col_tiles = n_col * stretch // edge, n_row * stretch // edge
    parts = 8 if slots % 8 == 0 else 1
    dense = (n_col, stretch, n_row * stretch)
    pieces = stretch // edge
    cut = (pieces, quarter, stretch // pieces)
    block = (quarter, stretch)
    vmem = pl.BlockSpec(memory_space=pltpu.VMEM)
    smem = pl.BlockSpec(memory_space=pltpu.SMEM)
    dma = pltpu.SemaphoreType.DMA
    piece = (peers, quarter // peers, width)
    n_y = n_row // 2
    results = pl.pallas_call(
        functools.partial(layer_kernel, n_row, n_col, n_rep),
        out_shape=(
            jax.ShapeDtypeStruct(block, F32),
            jax.ShapeDtypeStruct(block, F32),
            jax.ShapeDtypeStruct((quarter, width), F32),
        ),
        in_specs=[smem] * 2 + [vmem] * 2 + [pl.BlockSpec(memory_space=pltpu.HBM)] * 4,
        out_specs=(vmem,) * 3,
        scratch_shapes=[
            pltpu.VMEM((1, slots), jnp.int32),
            pltpu.VMEM((1, row_tiles * col_tiles), jnp.int32),
            pltpu.SMEM((1, slots), jnp.int32),
            pltpu.SMEM((1, row_tiles * col_tiles), jnp.int32),
            pltpu.VMEM(tile_values.shape, F32),
            pltpu.VMEM((slots + 1, edge, edge), F32),
            pltpu.VMEM(weight.shape, F32),
            pltpu.VMEM(dense, BF16),
            pltpu.VMEM(dense, BF16),
            pltpu.VMEM((n_row * stretch, 2 * quarter), BF16),
            pltpu.VMEM((n_row, *block), F32),
            pltpu.VMEM((n_rep, 1, *block), F32),
            pltpu.VMEM((n_rep, *cut), F32),
            pltpu.VMEM((n_col, *cut), F32),
            pltpu.VMEM((n_col, *cut), F32),
            pltpu.VMEM((n_rep * quarter, stretch), F32),
            pltpu.VMEM((n_col, *cut), F32),
            pltpu.VMEM((n_row, *block), F32),
            pltpu.VMEM((n_y, *block), F32),
            pltpu.VMEM((n_y, *block), F32),
            pltpu.VMEM(piece, F32),
            pltpu.VMEM(piece, F32),
            pltpu.VMEM(piece, F32),
            dma((2,)), dma((3,)), dma((parts,)),
            dma((n_row,)), dma((n_row,)),
            dma((2, n_rep, 1)), dma((n_rep, 1)),
            dma((2, n_rep, pieces)), dma((n_rep, pieces)),
            dma((n_col, pieces)), dma((n_col, pieces)),
            dma((n_col, pieces)), dma((n_col, pieces)),
            dma((n_y,)), dma((n_y,)),
            dma((n_y,)), dma((n_y,)),
            dma((peers,)), dma((peers,)),
            dma((peers,)), dma((peers,)),
        ],
        compiler_params=pltpu.CompilerParams(
            collective_id=0, has_side_effects=True, vmem_limit_bytes=56 * 2**20
        ),
    )(tile_kind, tile_count, tile_row, tile_col, features, weight, cotangent, tile_values)
    return leave(results)


def tile_terms(source, values, from_tile, to_tile, tile_kinds, live_weight, dest_tiles, transposed):
    feat_width = source.shape[0]
    tile_edge = values.shape[1]
    tiled = source.reshape(feat_width, source.shape[1] // tile_edge, tile_edge)
    picked = jnp.take(tiled, from_tile, axis=1)
    chosen = jnp.take(values, tile_kinds, axis=0)
    if transposed:
        products = jnp.einsum("fga,gab->fgb", picked, chosen, precision=lax.Precision.HIGHEST)
    else:
        products = jnp.einsum("fgb,gab->fga", picked, chosen, precision=lax.Precision.HIGHEST)
    onehot = (to_tile[:, None] == jnp.arange(dest_tiles, dtype=jnp.int32)[None, :]).astype(
        jnp.float32
    )
    onehot = onehot * live_weight[:, None]
    spread = jnp.einsum("fgt,gd->fdt", products, onehot, precision=lax.Precision.HIGHEST)
    return spread.reshape(feat_width, dest_tiles * tile_edge)


def aggregate(source, values, from_tile, to_tile, tile_kinds, live_count, dest_tiles, transposed):
    slot_total = tile_kinds.shape[0]
    live_weight = (jnp.arange(slot_total, dtype=jnp.int32) < live_count).astype(jnp.float32)
    return tile_terms(
        source, values, from_tile, to_tile, tile_kinds, live_weight, dest_tiles, transposed
    )


def local(features, weight, cotangent, tile_values, tile_row, tile_col, tile_kind, tile_count):
    n_rowdev = lax.axis_size("row")
    n_coldev = lax.axis_size("col")
    n_repdev = lax.axis_size("rep")
    quarter, stretch_len = features.shape
    nodes = n_rowdev * n_coldev
    if (
        n_rowdev * n_coldev * stretch_len * stretch_len * 4 <= DENSE_BYTES
        and n_rowdev % 2 == 0
        and n_coldev > 1
        and n_repdev > 1
        and quarter % (8 * nodes) == 0
        and tile_values.size * 4 <= DENSE_BYTES
    ):
        return fused(
            n_rowdev, n_coldev, n_repdev, features, weight, cotangent, tile_values,
            tile_row, tile_col, tile_kind, tile_count,
        )
    own_rows = lax.dynamic_slice_in_dim(weight, lax.axis_index("rep") * quarter, quarter, 0)
    tile_edge = tile_values.shape[1]
    live_count = tile_count[0]
    row_tiles = n_coldev * stretch_len // tile_edge
    col_tiles = n_rowdev * stretch_len // tile_edge
    mixed = lax.psum_scatter(
        lax.dot_general(
            own_rows,
            features,
            (((0,), (0,)), ((), ())),
            precision=lax.Precision.HIGHEST,
            preferred_element_type=jnp.float32,
        ),
        "rep",
        scatter_dimension=0,
        tiled=True,
    )
    column_block = lax.all_gather(mixed, "row", axis=1, tiled=True)
    partial_value = aggregate(
        column_block, tile_values, tile_col, tile_row, tile_kind, live_count, row_tiles, False
    )
    summed = lax.psum_scatter(partial_value, "col", scatter_dimension=1, tiled=True)
    output, pullback = jax.vjp(lambda v: jax.nn.gelu(v, approximate=True), summed)
    (grad_pre,) = pullback(cotangent)
    row_block = lax.all_gather(grad_pre, "col", axis=1, tiled=True)
    partial_back = aggregate(
        row_block, tile_values, tile_row, tile_col, tile_kind, live_count, col_tiles, True
    )
    grad_mixed = lax.psum_scatter(partial_back, "row", scatter_dimension=1, tiled=True)
    whole = lax.all_gather(grad_mixed, "rep", axis=0, tiled=True)
    input_grad = jnp.dot(
        own_rows, whole, preferred_element_type=jnp.float32, precision=lax.Precision.HIGHEST
    )
    weight_part = lax.dot_general(
        features,
        whole,
        (((1,), (1,)), ((), ())),
        precision=lax.Precision.HIGHEST,
        preferred_element_type=jnp.float32,
    )
    node_total = stretch_len * n_rowdev * n_coldev
    weight_grad = lax.psum(weight_part * float(node_total) ** (-0.5), ("row", "col"))
    return (output, input_grad, weight_grad)


def solution(mesh):
    return jax.shard_map(
        local,
        mesh=mesh,
        in_specs=(
            P("rep", ("col", "row")),
            P(),
            P("rep", ("row", "col")),
            P(("row", "col"), None, None),
            P(("row", "col")),
            P(("row", "col")),
            P(("row", "col")),
            P(("row", "col")),
        ),
        out_specs=(P("rep", ("row", "col")), P("rep", ("col", "row")), P("rep", None)),
        check_vma=False,
    )
```
